32 devices in a mesh: docs: 16 (over z, y, x), heads: 2 (over core).
Axes of the slice: x: 2, y: 2, z: 4, core: 2. Of those that a mesh axis runs over, the one named last changes fastest.
Arguments:
- tokens: bfloat16 [32768, 768], P('docs'), may hold values from -6 to 6
- grad_out: float32 [32768, 768], P('docs'), may hold values from -6 to 6
- live_tokens: int32 [16], P('docs'), may hold values from 1024 to 2048, as said below
- w_qkv: bfloat16 [768, 3, 768], P(None, None, 'heads'), may hold values from -0.21875 to 0.21875
- b_qv: float32 [2, 768], P(None, 'heads'), may hold values from -3 to 3
- w_out: bfloat16 [768, 768], P('heads'), may hold values from -0.875 to 0.875
- b_out: float32 [768], replicated, may hold values from -3 to 3
- gain_one: float32 [768], replicated, may hold values from 0.25 to 1.75
- shift_one: float32 [768], replicated, may hold values from -3 to 3
- w_up: bfloat16 [768, 3072], P(None, 'heads'), may hold values from -0.21875 to 0.21875
- b_up: float32 [3072], P('heads'), may hold values from -3 to 3
- w_down: bfloat16 [3072, 768], P('heads'), may hold values from -0.15625 to 0.15625
- b_down: float32 [768], replicated, may hold values from -3 to 3
- gain_two: float32 [768], replicated, may hold values from 0.25 to 1.75
- shift_two: float32 [768], replicated, may hold values from -3 to 3
Outputs:
- layer_out: float32 [32768, 768], P('docs')
- d_tokens: float32 [32768, 768], P('docs')
- d_w_qkv: float32 [768, 3, 768], P('docs', None, 'heads')
- d_b_qv: float32 [2, 768], P(None, 'heads')
- d_w_out: float32 [768, 768], P('heads', 'docs')
- d_b_out: float32 [768], replicated
- d_gain_one: float32 [768], replicated
- d_shift_one: float32 [768], replicated
- d_w_up: float32 [768, 3072], P('docs', 'heads')
- d_b_up: float32 [3072], P('heads')
- d_w_down: float32 [3072, 768], P('heads', 'docs')
- d_b_down: float32 [768], replicated
- d_gain_two: float32 [768], replicated
- d_shift_two: float32 [768], replicated
The draws below stay inside these ranges and needn't reach their ends.
Inputs may be any that keep to these rules, and one draw needn't show every extreme that they name: `live_tokens`: live tokens of each group; slots from there on are padding. Some group holds exactly 2048 and some exactly 1024.
All inputs are finite; a program needn't handle non-finite values.
Results may differ from the reference program's by a relative error of at most 0.02.
The reference program's roundings to bfloat16 on the way count: a program that leaves them out, or rounds other values in their place, can miss the bound.
Values may be sent and summed in bfloat16 or wider, within the bound.
No kernel may reach another device: no remote copies, remote signals or barrier semaphores. Data moves between devices by JAX's collectives and lax.ppermute only.
A program may use at most 192 MiB of HBM per device.

```python
import jax
import jax.numpy as jnp
from jax import lax

D = 768
HEAD_DIM = 64
FF = 3072
SEG = 128
TOK_DEV = 2048
GROUPS = 16
TOKENS = 32768
N_HEADS = 2


def draw_live_tokens(key, part):
    key = jax.random.fold_in(key, 7)
    first_key, second_key = jax.random.split(key)
    counts = jax.random.randint(first_key, (GROUPS,), TOK_DEV // 2, TOK_DEV + 1)
    order = jax.random.permutation(second_key, GROUPS)
    counts = counts.at[order[0]].set(TOK_DEV)
    counts = counts.at[order[1]].set(TOK_DEV // 2)
    return counts.astype(jnp.int32)


def raised(drawn, key, source, target, shards_of, factor):
    def block_of(dim):
        return (jnp.arange(drawn.shape[dim]) // (drawn.shape[dim] // shards_of)).reshape((-1,) + (1,) * (drawn.ndim - 1 - dim))

    one_side = jax.random.permutation(key, shards_of)[block_of(target)]
    other_side = (block_of(target) + shards_of // 2) % shards_of
    return jnp.where((block_of(source) == one_side) | (block_of(source) == other_side), factor * drawn, drawn)


def level_of(rng, shape, cuts, smallest, high):
    level = 1.0
    for axis_at, blocks in cuts:
        heights = jax.random.uniform(jax.random.fold_in(jax.random.fold_in(rng, 6), axis_at), (blocks,), jnp.float32, smallest / len(cuts), high / len(cuts))
        level = level * jnp.repeat(jnp.exp(heights), shape[axis_at] // blocks).reshape((-1,) + (1,) * (len(shape) - 1 - axis_at))
    return level


def normal_values(key, extent, deviation, bound, cuts=(), kind=jnp.bfloat16):
    entries = jax.random.normal(key, extent, jnp.float32) * deviation
    if len(cuts) > 0:
        entries = level_of(key, extent, cuts, -0.22, 0.18) * entries
    return jnp.clip(entries, min=-bound, max=bound).astype(kind)


def gaussian_with(key, extent, scale, bound, shards, heavy, dtype=jnp.bfloat16):
    drawn = scale * jax.random.normal(key, extent, jnp.float32)
    if shards:
        drawn = drawn * level_of(key, extent, shards, -0.22, 0.18)
    return jnp.clip(raised(drawn, jax.random.fold_in(key, 3), *heavy), -bound, bound).astype(dtype)


def setup_inputs(seed: int = 0) -> dict:
    seeds = jax.random.split(jax.random.key(seed), 16)
    return {
        "tokens": gaussian_with(seeds[0], (TOKENS, D), 1.0, 6.0, ((0, 16),), (0, 1, 16, 2.0)),
        "grad_out": gaussian_with(seeds[1], (TOKENS, D), 1.0, 6.0, ((0, 16),), (0, 1, 16, 2.0), jnp.float32),
        "live_tokens": draw_live_tokens(jax.random.fold_in(seeds[15], 71), 0),
        "w_qkv": normal_values(seeds[3], (D, 3, D), D ** -0.5, 0.21875, ((2, 2),)),
        "b_qv": normal_values(seeds[4], (2, D), 0.5, 3.0, ((1, 2),), jnp.float32),
        "w_out": normal_values(seeds[5], (D, D), (D // 16) ** -0.5, 0.875, ((0, 2),)),
        "b_out": normal_values(seeds[6], (D,), 0.5, 3.0, (), jnp.float32),
        "gain_one": jnp.clip(1.0 + 0.15 * jax.random.normal(seeds[7], (D,), jnp.float32), 0.25, 1.75),
        "shift_one": normal_values(seeds[8], (D,), 0.5, 3.0, (), jnp.float32),
        "w_up": normal_values(seeds[9], (D, FF), D ** -0.5, 0.21875, ((1, 2),)),
        "b_up": normal_values(seeds[10], (FF,), 0.5, 3.0, ((0, 2),), jnp.float32),
        "w_down": normal_values(seeds[11], (FF, D), (FF // 2) ** -0.5, 0.15625, ((0, 2),)),
        "b_down": normal_values(seeds[12], (D,), 0.5, 3.0, (), jnp.float32),
        "gain_two": jnp.clip(1.0 + 0.15 * jax.random.normal(seeds[13], (D,), jnp.float32), 0.25, 1.75),
        "shift_two": normal_values(seeds[14], (D,), 0.5, 3.0, (), jnp.float32),
    }


@jax.custom_vjp
def low(v):
    return lax.optimization_barrier(v.astype(jnp.bfloat16)).astype(jnp.float32)

@jax.custom_vjp
def low_back(v):
    return v

def low_keep(v):
    return (low(v), None)

def low_pass(kept, grad):
    return (grad,)

def back_keep(v):
    return (v, None)

def back_low(kept, grad):
    return (low(grad),)
low.defvjp(low_keep, low_pass)
low_back.defvjp(back_keep, back_low)

def high_dot(first, second):
    return jnp.dot(first, second, precision=lax.Precision.HIGHEST, preferred_element_type=jnp.float32)

def layer_norm(values, gain, shift):
    center = values - lax.optimization_barrier(jnp.mean(values, -1, keepdims=True))
    spread = lax.optimization_barrier(jnp.mean(center * center, -1, keepdims=True))
    return center * lax.rsqrt(spread + 1e-05) * gain + shift

def gelu_exact(values):
    return 0.5 * values * (1.0 + jax.scipy.special.erf(values * 0.7071067811865476))

def forward(params, inputs, live):
    w_qkv, b_qv, w_out, b_out, gain_one, shift_one, w_up, b_up, w_down, b_down, gain_two, shift_two = params
    count_rows = inputs.shape[0]
    local_cols = D // N_HEADS
    local_hidden = FF // N_HEADS
    local_heads = local_cols // HEAD_DIM
    segments = count_rows // SEG
    scale = HEAD_DIM ** (-0.5)
    row_mask = lax.iota(jnp.int32, count_rows) < live
    key_bias = jnp.where(row_mask, 0.0, -30000.0).astype(jnp.float32).reshape(segments, 1, 1, SEG)
    shape_four = (segments, SEG, local_heads, HEAD_DIM)
    inputs_low = low(inputs)
    attn_sum = jnp.zeros((count_rows, D), jnp.float32)
    for group in range(N_HEADS):
        first = group * local_cols
        last = first + local_cols
        linear = high_dot(low_back(inputs_low), w_qkv[:, :, first:last].reshape(D, 3 * local_cols))
        linear = linear.reshape(count_rows, 3, local_cols)
        query = low(low_back(linear[:, 0] + b_qv[0, first:last])).reshape(shape_four)
        keys = low(low_back(linear[:, 1])).reshape(shape_four)
        values = low(low_back(linear[:, 2] + b_qv[1, first:last])).reshape(shape_four)
        scores = low_back(jnp.einsum('sqhd,skhd->shqk', query, keys, precision=lax.Precision.HIGHEST) * scale) + key_bias
        top_score = lax.optimization_barrier(jnp.max(scores, -1, keepdims=True))
        exp_scores = jnp.exp(scores - top_score)
        probs = low(exp_scores / lax.optimization_barrier(jnp.sum(exp_scores, -1, keepdims=True)))
        attended = jnp.einsum('shqk,skhd->sqhd', probs, values, precision=lax.Precision.HIGHEST)
        attended = low(low_back(attended.reshape(count_rows, local_cols)))
        attn_sum = attn_sum + low(high_dot(attended, w_out[first:last]))
    normed_one = layer_norm(inputs + low_back(attn_sum) + b_out, gain_one, shift_one)
    normed_low = low(normed_one)
    mlp_sum = jnp.zeros((count_rows, D), jnp.float32)
    for group in range(N_HEADS):
        first = group * local_hidden
        last = first + local_hidden
        pre = low_back(high_dot(low_back(normed_low), w_up[:, first:last]) + b_up[first:last])
        hidden = low(gelu_exact(pre))
        mlp_sum = mlp_sum + low(high_dot(hidden, w_down[first:last]))
    return layer_norm(normed_one + low_back(mlp_sum) + b_down, gain_two, shift_two)

def reference(tokens, grad_out, live_tokens, w_qkv, b_qv, w_out, b_out, gain_one, shift_one, w_up, b_up, w_down, b_down, gain_two, shift_two):
    params = tuple((item.astype(jnp.float32) for item in (w_qkv, b_qv, w_out, b_out, gain_one, shift_one, w_up, b_up, w_down, b_down, gain_two, shift_two)))
    token_groups = tokens.astype(jnp.float32).reshape(GROUPS, TOK_DEV, D)
    grad_groups = grad_out.astype(jnp.float32).reshape(GROUPS, TOK_DEV, D)

    def one_group(totals, item):
        inputs, cotangent, live = item
        result, backward = jax.vjp(lambda weights, values: forward(weights, values, live), params, inputs)
        row_mask = (lax.iota(jnp.int32, TOK_DEV) < live)[:, None]
        d_params, d_inputs = backward(jnp.where(row_mask, cotangent, 0.0))
        totals = jax.tree.map(lambda left, right: left + right, totals, d_params)
        return (totals, (result, d_inputs))
    zeros = jax.tree.map(jnp.zeros_like, params)
    totals, (results, d_inputs) = lax.scan(one_group, zeros, (token_groups, grad_groups, live_tokens))
    return (results.reshape(TOKENS, D), d_inputs.reshape(TOKENS, D), totals[0], totals[1], totals[2], totals[3], totals[4], totals[5], totals[6], totals[7], totals[8], totals[9], totals[10], totals[11])
```

```python
import functools

import jax
import jax.numpy as jnp
from jax import lax
from jax.experimental import pallas as pl
from jax.experimental.pallas import tpu as pltpu
from jax.sharding import PartitionSpec as P

HEAD_DIM = 64
SEG = 128
EPS = 1e-05
LANES = 128
F32 = jnp.float32
LOW = jnp.bfloat16
OWN = jnp.float32
BWD_CHUNK = 768
VMEM_LIMIT = 60 * 1024 * 1024


def mm(first, second):
    return jnp.dot(first, second, preferred_element_type=F32)


def mm_nt(first, second):
    return lax.dot_general(first, second, (((1,), (1,)), ((), ())), preferred_element_type=F32)


def mm_tn(first, second):
    return lax.dot_general(first, second, (((0,), (0,)), ((), ())), preferred_element_type=F32)


def fold_rows(values):
    rows, width = values.shape
    return jnp.sum(values.reshape(rows // 8, 8, width), 0)


def gelu_pair(pre):
    below = 0.5 + 0.5 * lax.erf(pre * 0.7071067811865476)
    bell = jnp.exp2(pre * pre * (-0.5 * 1.4426950408889634))
    return pre * below, below + pre * bell * 0.3989422804014327


def const_spec(shape):
    zeros = (0,) * len(shape)
    return pl.BlockSpec(shape, lambda i, s: zeros, pipeline_mode=pl.Buffered(1))


def row_spec(block, width):
    return pl.BlockSpec((block, width), lambda i, s: (i, 0))


def params():
    return pltpu.CompilerParams(dimension_semantics=("arbitrary",), vmem_limit_bytes=VMEM_LIMIT)


def attn_fwd_kernel(block, rows, s_ref, x_ref, w_ref, b_ref, qkv_ref, p_ref, a_ref):
    cols = w_ref.shape[2]
    x = x_ref[...]
    q = ((mm(x, w_ref[0]) + b_ref[0:1, :]) * (HEAD_DIM**-0.5)).astype(LOW)
    k = mm(x, w_ref[1]).astype(LOW)
    v = (mm(x, w_ref[2]) + b_ref[1:2, :]).astype(LOW)
    qkv_ref[:, 0:cols] = q
    qkv_ref[:, cols : 2 * cols] = k
    qkv_ref[:, 2 * cols : 3 * cols] = v
    left = lax.broadcasted_iota(jnp.int32, (SEG, LANES), 1) < HEAD_DIM
    first_slot = s_ref[0] * rows + pl.program_id(0) * block
    zero = jnp.zeros((), LOW)
    for seg in range(block // SEG):
        at = slice(seg * SEG, (seg + 1) * SEG)
        slots = lax.broadcasted_iota(jnp.int32, (SEG, 2 * SEG), 0) + (first_slot + seg * SEG)
        bias = jnp.where(slots < s_ref[1], 0.0, -30000.0)
        for pair in range(cols // LANES):
            lanes = slice(pair * LANES, (pair + 1) * LANES)
            qp, kp, vp = q[at, lanes], k[at, lanes], v[at, lanes]
            both = jnp.concatenate([jnp.where(left, qp, zero), jnp.where(left, zero, qp)], 0)
            scores = mm_nt(kp, both) + bias
            top = jnp.max(scores, 0, keepdims=True)
            grown = jnp.exp(scores - top)
            probs = (grown * (1.0 / jnp.sum(grown, 0, keepdims=True))).astype(LOW)
            p_ref[at, 2 * pair * SEG : 2 * (pair + 1) * SEG] = probs
            stacked = jnp.concatenate([probs[:, :SEG], probs[:, SEG:]], 0)
            values = jnp.concatenate([jnp.where(left, vp, zero), jnp.where(left, zero, vp)], 0)
            a_ref[at, lanes] = mm_tn(stacked, values).astype(LOW)


def attn_fwd(scal, tokens, w, b, rows, block):
    cols = w.shape[2]
    width = tokens.shape[1]
    steps = rows // block
    heads = cols // HEAD_DIM
    return pl.pallas_call(
        functools.partial(attn_fwd_kernel, block, rows),
        grid_spec=pltpu.PrefetchScalarGridSpec(
            num_scalar_prefetch=1,
            grid=(steps,),
            in_specs=[
                pl.BlockSpec((block, width), lambda i, s: (s[0] * steps + i, 0)),
                const_spec(w.shape),
                const_spec(b.shape),
            ],
            out_specs=[row_spec(block, 3 * cols), row_spec(block, heads * SEG), row_spec(block, cols)],
        ),
        out_shape=[
            jax.ShapeDtypeStruct((rows, 3 * cols), LOW),
            jax.ShapeDtypeStruct((rows, heads * SEG), LOW),
            jax.ShapeDtypeStruct((rows, cols), LOW),
        ],
        compiler_params=params(),
        cost_estimate=pl.CostEstimate(
            flops=2 * rows * width * 3 * cols + 8 * rows * SEG * cols,
            bytes_accessed=rows * (width + 4 * cols + heads * SEG) * 2 + w.size * 2,
            transcendentals=rows * heads * SEG,
        ),
        name="attn_fwd",
    )(scal, tokens, w, b)


def spread(grad, out_ref, table, parts):
    if out_ref.shape[0] == 1:
        out_ref[0] = grad
        return
    share = grad.shape[0] // parts
    for part in range(parts):
        out_ref[table(part)] = grad[part * share : (part + 1) * share]


def slots_of(width, parts):
    share = width // parts
    return (parts, share) if share % 16 == 0 else (1, width)


def arrange(grad, table, parts):
    if grad.shape[0] == parts:
        return grad
    spots = jnp.zeros((parts,), jnp.int32).at[table].set(jnp.arange(parts, dtype=jnp.int32))
    return jnp.take(grad.reshape(parts, -1, grad.shape[2]), spots, axis=0)


class Fetch:
    def __init__(self, sources, targets, sems):
        self.copies = [pltpu.make_async_copy(s, t, sems.at[i]) for i, (s, t) in enumerate(zip(sources, targets))]

    def start(self):
        @pl.when(pl.program_id(0) == 0)
        def _():
            for copy in self.copies:
                copy.start()

    def wait(self, *which):
        @pl.when(pl.program_id(0) == 0)
        def _():
            for i in which:
                self.copies[i].wait()


ANY = pl.BlockSpec(memory_space=pl.ANY)


def ffn_fwd_kernel(
    block, rows, chunk, parts, steps,
    s_ref, x_ref, g_ref, ao_ref, at_ref, bu_ref, vec_ref, woo_hbm, wot_hbm, wuo_hbm, wut_hbm, wdo_hbm, wdt_hbm,
    gp_ref, low_ref, hat_ref, rs_ref, out_ref, own_ref, dmlp_ref, sums_ref, gt_ref, go_ref,
    woo_ref, wot_ref, wuo_ref, wut_ref, wdo_ref, wdt_ref, sems, hid_ref, all_ref,
):
    step = pl.program_id(0)
    half = wuo_ref.shape[1]
    fetch = Fetch(
        (woo_hbm, wot_hbm, wuo_hbm, wdo_hbm, wut_hbm, wdt_hbm),
        (woo_ref, wot_ref, wuo_ref, wdo_ref, wut_ref, wdt_ref),
        sems,
    )
    fetch.start()

    @pl.when(step == 0)
    def _():
        sums_ref[...] = jnp.zeros_like(sums_ref)

    @pl.when(step < steps)
    def _():
        b_out, gain_one, shift_one = vec_ref[0:1, :], vec_ref[1:2, :], vec_ref[2:3, :]
        b_down, gain_two, shift_two = vec_ref[3:4, :], vec_ref[4:5, :], vec_ref[5:6, :]
        fetch.wait(0, 1)
        h1 = x_ref[...].astype(F32) + mm(ao_ref[...], woo_ref[...]) + mm(at_ref[...], wot_ref[...]) + b_out
        center = h1 - jnp.mean(h1, -1, keepdims=True)
        scale = lax.rsqrt(jnp.mean(center * center, -1, keepdims=True) + EPS)
        hat = center * scale
        normed = hat * gain_one + shift_one
        hat_ref[...] = hat.astype(LOW)
        rs_ref[...] = jnp.broadcast_to(scale, rs_ref.shape)
        low = normed.astype(LOW)
        low_ref[...] = low
        total = normed + b_down
        mine = pl.ds(pl.multiple_of(step * block, block), block)
        for side, (wu, wd) in enumerate(((wuo_ref, wdo_ref), (wut_ref, wdt_ref))):
            fetch.wait(2 + 2 * side, 3 + 2 * side)
            for start in range(0, half, chunk):
                at = slice(start, start + chunk)
                where = slice(side * half + start, side * half + start + chunk)
                pre = mm(low, wu[:, at]) + bu_ref[:, where]
                hidden, slope = gelu_pair(pre)
                hidden = hidden.astype(LOW)
                hid_ref[mine, where] = hidden
                gp_ref[:, where] = slope.astype(LOW)
                total = total + mm(hidden, wd[at, :])
        center = total - jnp.mean(total, -1, keepdims=True)
        scale = lax.rsqrt(jnp.mean(center * center, -1, keepdims=True) + EPS)
        hat = center * scale
        result = hat * gain_two + shift_two
        out_ref[...] = result
        own_ref[...] = result.astype(own_ref.dtype)
        slots = lax.broadcasted_iota(jnp.int32, (block, 1), 0) + (s_ref[0] * rows + step * block)
        cot = jnp.where(slots < s_ref[1], g_ref[...], 0.0)
        inner = cot * gain_two
        d_h2 = scale * (
            inner - jnp.mean(inner, -1, keepdims=True) - hat * jnp.mean(inner * hat, -1, keepdims=True)
        )
        low = d_h2.astype(LOW)
        dmlp_ref[...] = low
        all_ref[mine, :] = low
        sums_ref[0:8, :] += fold_rows(cot * hat)
        sums_ref[8:16, :] += fold_rows(cot)
        sums_ref[16:24, :] += fold_rows(d_h2)

    wide = gt_ref.shape[2]
    for side, grad_ref in ((1, gt_ref), (0, go_ref)):
        for piece in range(half // wide):
            at = side * half + piece * wide

            @pl.when(step == steps + (1 - side) * (half // wide) + piece)
            def _():
                grad = mm_tn(all_ref[...], hid_ref[:, at : at + wide]).astype(LOW)
                spread(grad, grad_ref, lambda part: s_ref[2 + side * parts + part], parts)


def ffn_fwd(scal, tokens, grad_out, att, w_out, w_up, b_up, w_down, vec, rows, block, chunk, wide, parts):
    width = tokens.shape[1]
    steps = rows // block
    half = w_up[0].shape[1]
    pieces = half // wide
    cols = att[0].shape[1]
    last = steps - 1
    row = lambda i: jnp.minimum(i, last)
    mine = lambda i, s: (s[0] * steps + row(i), 0)
    rows_of = lambda w: pl.BlockSpec((block, w), lambda i, s: (row(i), 0))
    outs = [(2 * half, LOW), (width, LOW), (width, LOW), (LANES, F32)]
    lead = slots_of(width, parts)
    weights = [*w_out, *w_up, *w_down]
    grads = jax.ShapeDtypeStruct((*lead, half), LOW)
    clamp = lambda v: jnp.clip(v, 0, pieces - 1)
    return pl.pallas_call(
        functools.partial(ffn_fwd_kernel, block, rows, chunk, parts, steps),
        grid_spec=pltpu.PrefetchScalarGridSpec(
            num_scalar_prefetch=1,
            grid=(steps + 2 * pieces,),
            in_specs=[pl.BlockSpec((block, width), mine), pl.BlockSpec((block, width), mine), rows_of(cols), rows_of(cols)]
            + [const_spec(b_up.shape), const_spec(vec.shape)]
            + [ANY] * 6,
            out_specs=[rows_of(w) for w, _ in outs]
            + [pl.BlockSpec((block, width), mine), rows_of(width), rows_of(width)]
            + [pl.BlockSpec((24, width), lambda i, s: (0, 0))]
            + [
                pl.BlockSpec((*lead, wide), lambda i, s: (0, 0, clamp(i - steps))),
                pl.BlockSpec((*lead, wide), lambda i, s: (0, 0, clamp(i - steps - pieces))),
            ],
            scratch_shapes=[pltpu.VMEM(w.shape, LOW) for w in weights]
            + [pltpu.SemaphoreType.DMA((6,)), pltpu.VMEM((rows, 2 * half), LOW), pltpu.VMEM((rows, width), LOW)],
        ),
        out_shape=[jax.ShapeDtypeStruct((rows, w), t) for w, t in outs]
        + [
            jax.ShapeDtypeStruct((2 * rows, width), F32),
            jax.ShapeDtypeStruct((rows, width), OWN),
            jax.ShapeDtypeStruct((rows, width), LOW),
            jax.ShapeDtypeStruct((24, width), F32),
            grads,
            grads,
        ],
        compiler_params=params(),
        cost_estimate=pl.CostEstimate(
            flops=2 * rows * width * (6 * half + 2 * cols),
            bytes_accessed=rows * (4 * half + 24 * width),
            transcendentals=rows * 2 * half,
        ),
        name="ffn_fwd",
    )(scal, tokens, grad_out, *att, b_up, vec, *weights)


def ffn_bwd_kernel(
    block, chunk, parts, steps,
    s_ref, dmlp_ref, gp_ref, hat_ref, rs_ref, low_ref, ao_ref, at_ref, vec_ref,
    woo_hbm, wot_hbm, wuo_hbm, wut_hbm, wdo_hbm, wdt_hbm,
    dh1_ref, dao_ref, dat_ref, sums_ref, bup_ref, gt_ref, go_ref, ot_ref, oo_ref,
    woo_ref, wot_ref, wuo_ref, wut_ref, wdo_ref, wdt_ref, sems, dpre_ref, dbr_ref,
):
    step = pl.program_id(0)
    half = wuo_ref.shape[1]
    fetch = Fetch(
        (wdo_hbm, wuo_hbm, wdt_hbm, wut_hbm, woo_hbm, wot_hbm),
        (wdo_ref, wuo_ref, wdt_ref, wut_ref, woo_ref, wot_ref),
        sems,
    )
    fetch.start()

    @pl.when(step == 0)
    def _():
        sums_ref[...] = jnp.zeros_like(sums_ref)
        bup_ref[...] = jnp.zeros_like(bup_ref)

    @pl.when(step < steps)
    def _():
        mine = pl.ds(pl.multiple_of(step * block, block), block)
        d_mlp = dmlp_ref[...]
        total = d_mlp.astype(F32)
        for side, (wu, wd) in enumerate(((wuo_ref, wdo_ref), (wut_ref, wdt_ref))):
            fetch.wait(2 * side, 2 * side + 1)
            for start in range(0, half, chunk):
                at = slice(start, start + chunk)
                where = slice(side * half + start, side * half + start + chunk)
                d_hidden = mm_nt(d_mlp, wd[at, :])
                d_pre = (d_hidden * gp_ref[:, where].astype(F32)).astype(LOW)
                dpre_ref[mine, where] = d_pre
                bup_ref[:, where] += fold_rows(d_pre.astype(F32))
                total = total + mm_nt(d_pre, wu[:, at])
        hat = hat_ref[...].astype(F32)
        inner = total * vec_ref[1:2, :]
        scale = rs_ref[:, 0:1]
        d_h1 = scale * (
            inner - jnp.mean(inner, -1, keepdims=True) - hat * jnp.mean(inner * hat, -1, keepdims=True)
        )
        sums_ref[0:8, :] += fold_rows(total * hat)
        sums_ref[8:16, :] += fold_rows(total)
        sums_ref[16:24, :] += fold_rows(d_h1)
        dh1_ref[...] = d_h1
        low = d_h1.astype(LOW)
        dbr_ref[mine, :] = low
        fetch.wait(4, 5)
        dao_ref[...] = mm_nt(low, woo_ref[...]).astype(LOW)
        dat_ref[...] = mm_nt(low, wot_ref[...]).astype(LOW)

    wide = gt_ref.shape[2]
    pieces = half // wide
    for side, grad_ref in ((1, gt_ref), (0, go_ref)):
        for piece in range(pieces):
            at = side * half + piece * wide

            @pl.when(step == steps + (1 - side) * pieces + piece)
            def _():
                grad = mm_tn(low_ref[...], dpre_ref[:, at : at + wide]).astype(LOW)
                spread(grad, grad_ref, lambda part: s_ref[2 + side * parts + part], parts)

    @pl.when(step == steps + 2 * pieces)
    def _():
        for side, (att_ref, grad_ref) in enumerate(((ao_ref, oo_ref), (at_ref, ot_ref))):
            grad = mm_tn(dbr_ref[...], att_ref[...]).astype(LOW)
            spread(grad, grad_ref, lambda part: s_ref[2 + side * parts + part], parts)


def ffn_bwd(scal, d_mlp, slope, hat, scale, normed_low, att, w_out, w_up, w_down, vec, block, chunk, wide, parts):
    rows, width = d_mlp.shape
    steps = rows // block
    half = w_up[0].shape[1]
    pieces = half // wide
    cols = w_out[0].shape[0]
    last = steps - 1
    rows_of = lambda w: pl.BlockSpec((block, w), lambda i, s: (jnp.minimum(i, last), 0))
    fixed = lambda shape: pl.BlockSpec(shape, lambda i, s: (0,) * len(shape))
    moving = [d_mlp, slope, hat, scale]
    consts = [normed_low, *att, vec]
    weights = [*w_out, *w_up, *w_down]
    outs = [(width, F32), (cols, LOW), (cols, LOW)]
    lead = slots_of(width, parts)
    grads = jax.ShapeDtypeStruct((*lead, half), LOW)
    narrow = jax.ShapeDtypeStruct((*lead, cols), LOW)
    clamp = lambda v: jnp.clip(v, 0, pieces - 1)
    return pl.pallas_call(
        functools.partial(ffn_bwd_kernel, block, chunk, parts, steps),
        grid_spec=pltpu.PrefetchScalarGridSpec(
            num_scalar_prefetch=1,
            grid=(steps + 2 * pieces + 1,),
            in_specs=[rows_of(m.shape[1]) for m in moving] + [const_spec(c.shape) for c in consts] + [ANY] * 6,
            out_specs=[rows_of(w) for w, _ in outs]
            + [fixed((24, width)), fixed((8, 2 * half))]
            + [
                pl.BlockSpec((*lead, wide), lambda i, s: (0, 0, clamp(i - steps))),
                pl.BlockSpec((*lead, wide), lambda i, s: (0, 0, clamp(i - steps - pieces))),
                fixed((*lead, cols)),
                fixed((*lead, cols)),
            ],
            scratch_shapes=[pltpu.VMEM(w.shape, LOW) for w in weights]
            + [pltpu.SemaphoreType.DMA((6,)), pltpu.VMEM((rows, 2 * half), LOW), pltpu.VMEM((rows, width), LOW)],
        ),
        out_shape=[jax.ShapeDtypeStruct((rows, w), t) for w, t in outs]
        + [jax.ShapeDtypeStruct((24, width), F32), jax.ShapeDtypeStruct((8, 2 * half), F32), grads, grads, narrow, narrow],
        compiler_params=params(),
        cost_estimate=pl.CostEstimate(
            flops=2 * rows * width * (6 * half + 4 * cols),
            bytes_accessed=rows * (4 * half + 20 * width),
            transcendentals=0,
        ),
        name="ffn_bwd",
    )(scal, *moving, *consts, *weights)


def attn_bwd_kernel(block, side, parts, steps, s_ref, x_ref, qkv_ref, p_ref, da_ref, dl_ref, sums_ref, grad_ref, all_ref):
    cols = da_ref.shape[1]
    step = pl.program_id(0)

    @pl.when(step == 0)
    def _():
        sums_ref[...] = jnp.zeros_like(sums_ref)

    left = lax.broadcasted_iota(jnp.int32, (SEG, LANES), 1) < HEAD_DIM
    zero = jnp.zeros((), LOW)

    def split(values):
        return jnp.concatenate([jnp.where(left, values, zero), jnp.where(left, zero, values)], 0)

    @pl.when(step < steps)
    def _():
        for pair in range(cols // LANES):
            lanes = slice(pair * LANES, (pair + 1) * LANES)
            k_lanes = slice(cols + pair * LANES, cols + (pair + 1) * LANES)
            v_lanes = slice(2 * cols + pair * LANES, 2 * cols + (pair + 1) * LANES)
            sum_q = jnp.zeros((8, LANES), F32)
            sum_v = jnp.zeros((8, LANES), F32)
            for seg in range(block // SEG):
                at = slice(seg * SEG, (seg + 1) * SEG)
                qp, kp, vp, dap = qkv_ref[at, lanes], qkv_ref[at, k_lanes], qkv_ref[at, v_lanes], da_ref[at, lanes]
                probs = p_ref[at, 2 * pair * SEG : 2 * (pair + 1) * SEG]
                da_split = split(dap)
                d_probs = mm_nt(vp, da_split)
                wide = probs.astype(F32)
                d_scores = (wide * (d_probs - jnp.sum(wide * d_probs, 0, keepdims=True))).astype(LOW)
                d_v = mm(probs, da_split).astype(LOW)
                d_k = mm(d_scores, split(qp)).astype(LOW)
                stacked = jnp.concatenate([d_scores[:, :SEG], d_scores[:, SEG:]], 0)
                d_q = (mm_tn(stacked, split(kp)) * (HEAD_DIM**-0.5)).astype(LOW)
                dl_ref[at, lanes] = d_q
                dl_ref[at, k_lanes] = d_k
                dl_ref[at, v_lanes] = d_v
                sum_q += fold_rows(d_q.astype(F32))
                sum_v += fold_rows(d_v.astype(F32))
            sums_ref[:, lanes] += sum_q
            sums_ref[:, k_lanes] += sum_v
        all_ref[pl.ds(pl.multiple_of(step * block, block), block), :] = dl_ref[...]

    wide = grad_ref.shape[2]
    for piece in range(3 * cols // wide):

        @pl.when(step == steps + piece)
        def _():
            grad = mm_tn(x_ref[...], all_ref[:, piece * wide : (piece + 1) * wide]).astype(LOW)
            spread(grad, grad_ref, lambda part: s_ref[2 + side * parts + part], parts)


def attn_bwd(scal, tokens, qkv, probs, d_att, side, block, wide, parts):
    rows, cols = d_att.shape
    width = tokens.shape[1]
    steps = rows // block
    pieces = 3 * cols // wide
    last = steps - 1
    rows_of = lambda w: pl.BlockSpec((block, w), lambda i, s: (jnp.minimum(i, last), 0))
    moving = [qkv, probs, d_att]
    lead = slots_of(width, parts)
    return pl.pallas_call(
        functools.partial(attn_bwd_kernel, block, side, parts, steps),
        grid_spec=pltpu.PrefetchScalarGridSpec(
            num_scalar_prefetch=1,
            grid=(steps + pieces,),
            in_specs=[pl.BlockSpec((rows, width), lambda i, s: (s[0], 0), pipeline_mode=pl.Buffered(1))]
            + [rows_of(m.shape[1]) for m in moving],
            out_specs=[
                rows_of(3 * cols),
                pl.BlockSpec((8, 2 * cols), lambda i, s: (0, 0)),
                pl.BlockSpec((*lead, wide), lambda i, s: (0, 0, jnp.clip(i - steps, 0, pieces - 1))),
            ],
            scratch_shapes=[pltpu.VMEM((rows, 3 * cols), LOW)],
        ),
        out_shape=[
            jax.ShapeDtypeStruct((rows, 3 * cols), LOW),
            jax.ShapeDtypeStruct((8, 2 * cols), F32),
            jax.ShapeDtypeStruct((*lead, 3 * cols), LOW),
        ],
        compiler_params=params(),
        cost_estimate=pl.CostEstimate(
            flops=16 * rows * SEG * cols * 2 + 6 * rows * width * cols,
            bytes_accessed=rows * (7 * cols + probs.shape[1]) * 2,
            transcendentals=0,
        ),
        name="attn_bwd",
    )(scal, tokens, *moving)


def d_tokens_kernel(s_ref, dh1_ref, dlo_ref, dlt_ref, wo_ref, wt_ref, out_ref, own_ref):
    cols = wo_ref.shape[2]
    total = dh1_ref[...]
    for d_lin, w in ((dlo_ref, wo_ref), (dlt_ref, wt_ref)):
        for kind in range(3):
            total = total + mm_nt(d_lin[:, kind * cols : (kind + 1) * cols], w[kind])
    out_ref[...] = total
    own_ref[...] = total


def d_tokens_of(scal, d_h1, d_lin, w_qkv, block):
    rows, width = d_h1.shape
    steps = rows // block
    wide = d_lin[0].shape[1]
    return pl.pallas_call(
        d_tokens_kernel,
        grid_spec=pltpu.PrefetchScalarGridSpec(
            num_scalar_prefetch=1,
            grid=(steps,),
            in_specs=[row_spec(block, width), row_spec(block, wide), row_spec(block, wide)]
            + [const_spec(w.shape) for w in w_qkv],
            out_specs=[pl.BlockSpec((block, width), lambda i, s: (s[0] * steps + i, 0)), row_spec(block, width)],
        ),
        out_shape=[jax.ShapeDtypeStruct((2 * rows, width), F32), jax.ShapeDtypeStruct((rows, width), F32)],
        compiler_params=params(),
        cost_estimate=pl.CostEstimate(
            flops=4 * rows * width * wide, bytes_accessed=rows * (12 * width + 4 * wide), transcendentals=0
        ),
        name="d_tokens",
    )(scal, d_h1, *d_lin, *w_qkv)


def place_kernel(s_ref, whole_ref, part_ref, out_ref):
    out_ref[...] = part_ref[...]


def place_other(scal, whole, part, block):
    rows, width = part.shape
    steps = rows // block
    return pl.pallas_call(
        place_kernel,
        grid_spec=pltpu.PrefetchScalarGridSpec(
            num_scalar_prefetch=1,
            grid=(steps,),
            in_specs=[pl.BlockSpec(memory_space=pl.ANY), row_spec(block, width)],
            out_specs=pl.BlockSpec((block, width), lambda i, s: ((1 - s[0]) * steps + i, 0)),
        ),
        out_shape=jax.ShapeDtypeStruct(whole.shape, F32),
        input_output_aliases={1: 0},
        compiler_params=params(),
        cost_estimate=pl.CostEstimate(flops=0, bytes_accessed=8 * rows * width, transcendentals=0),
        name="place_other",
    )(scal, whole, part)


def shards(
    n_docs, tokens, grad_out, live_tokens, w_qkv, b_qv, w_out, b_out, gain_one, shift_one, w_up, b_up, w_down, b_down,
    gain_two, shift_two,
):
    c = lax.axis_index("heads")
    me = lax.axis_index("docs")
    rows = tokens.shape[0] // 2
    bits = n_docs.bit_length() - 1
    orders = [list(range(bits)), [1, 0] + list(range(2, bits))]

    def step_pairs(stage):
        return [
            (d * 2 + h, (d ^ (1 << orders[h][stage])) * 2 + h) for d in range(n_docs) for h in range(2)
        ]

    def step(value, stage):
        return lax.ppermute(value, ("docs", "heads"), step_pairs(stage))

    def swap(value):
        return lax.ppermute(value, "heads", [(0, 1), (1, 0)])

    def table_for(core):
        away = jnp.arange(n_docs, dtype=jnp.int32) ^ me
        slots = []
        for order in orders:
            slot = jnp.zeros((n_docs,), jnp.int32)
            for place, bit in enumerate(order):
                slot = slot | (((away >> bit) & 1) << (bits - 1 - place))
            slots.append(slot)
        return jnp.where(core == 0, slots[0], slots[1])

    tables = (table_for(c), table_for(1 - c))
    scal = jnp.concatenate([c[None].astype(jnp.int32), live_tokens, *tables])

    w_qkv = jnp.transpose(w_qkv, (1, 0, 2))
    w_qkv2 = (w_qkv, swap(w_qkv))
    b_qv2 = (b_qv, swap(b_qv))
    w_out2 = (w_out, swap(w_out))
    w_up2 = (w_up, swap(w_up))
    w_down2 = (w_down, swap(w_down))
    b_up2 = jnp.concatenate([b_up, swap(b_up)])[None]
    vec = jnp.stack([b_out, gain_one, shift_one, b_down, gain_two, shift_two, b_out, b_out])

    def add(left, right):
        return (left.astype(F32) + right.astype(F32)).astype(LOW)

    def first_sum(pairs):
        half = n_docs // 2
        parts = [(arrange(own, tables[0], n_docs), arrange(swap(other), tables[0], n_docs)) for own, other in pairs]
        cut = lambda at: jnp.concatenate([add(own[at], other[at]) for own, other in parts], 2)
        return cut(slice(half, None)), cut(slice(None, half))

    def next_sum(keep, came):
        half = keep.shape[0] // 2
        if not half:
            return (keep.astype(F32) + came.astype(F32))[0]
        return add(keep[half:], came[half:]), add(keep[:half], came[:half])

    def after(value, *before):
        return lax.optimization_barrier((value, *before))[0]

    block = 256
    qkv, probs, att = [None] * 2, [None] * 2, [None] * 2
    for side in range(2):
        qkv[side], probs[side], att[side] = attn_fwd(scal, tokens, w_qkv2[side], b_qv2[side], rows, block)
    half = w_up.shape[1]
    slope, normed_low, hat, scale, layer_out, layer_own, d_mlp, sums_two, down_other, down_own = ffn_fwd(
        scal, tokens, grad_out, att, w_out2, w_up2, b_up2, w_down2, vec, rows, block, BWD_CHUNK, 768, n_docs
    )
    layer_out = place_other(scal, layer_out, swap(layer_own), block)
    send, keep = first_sum([(down_own, down_other)])
    down = [(send, keep)]
    came_down = step(send, 0)
    d_mlp = after(d_mlp, send)
    d_h1, d_att_own, d_att_other, sums_one, sums_up, up_other, up_own, out_other, out_own = ffn_bwd(
        scal, d_mlp, slope, hat, scale, normed_low, att, w_out2, w_up2, w_down2, vec, block, BWD_CHUNK, 768, n_docs
    )

    def run(send, keep, came=None):
        for stage in range(bits):
            if came is None:
                came = step(send, stage)
            if stage == bits - 1:
                return next_sum(keep, came)
            send, keep = next_sum(keep, came)
            came = None

    d_w_down = run(send, keep, came_down).T
    up = first_sum([(up_own, up_other), (out_own, out_other)])
    d_att_other = after(d_att_other, up[0])
    rest = run(*up)
    d_w_up, d_w_out = rest[:, :half], rest[:, half:].T
    cols = att[0].shape[1]
    d_lin_other, sums_other, lin_other = attn_bwd(scal, tokens, qkv[1], probs[1], d_att_other, 1, block, cols, n_docs)
    d_lin_own, sums_own, lin_own = attn_bwd(scal, tokens, qkv[0], probs[0], d_att_own, 0, block, cols, n_docs)
    lin = first_sum([(lin_own, lin_other)])
    d_w_qkv = run(*lin)
    d_h1 = after(d_h1, lin[0])
    d_tokens, d_tok_own = d_tokens_of(scal, d_h1, (d_lin_own, d_lin_other), w_qkv2, block)
    d_tokens = place_other(scal, d_tokens, swap(d_tok_own), block)

    width = tokens.shape[1]
    common = jnp.concatenate([jnp.sum(s.reshape(3, 8, width), 1).reshape(-1) for s in (sums_two, sums_one)])
    sums_up = jnp.sum(sums_up, 0)
    other = jnp.concatenate([sums_up[half:], jnp.sum(sums_other, 0)])
    own = jnp.concatenate([sums_up[:half], jnp.sum(sums_own, 0)])
    small = jnp.concatenate([common, own]) + swap(jnp.concatenate([common, other]))
    small = small.reshape(-1, LANES)
    for stage in range(bits):
        small = small + lax.ppermute(small, "docs", [(d, d ^ (1 << stage)) for d in range(n_docs)])
    small = small.reshape(-1)
    d_gain_two, d_shift_two, d_b_down, d_gain_one, d_shift_one, d_b_out = small[: 6 * width].reshape(6, width)
    d_b_up = small[6 * width : 6 * width + half]
    d_b_qv = small[6 * width + half :].reshape(2, cols)
    return (
        layer_out,
        d_tokens,
        jnp.transpose(d_w_qkv.reshape(-1, 3, cols), (0, 1, 2)),
        d_b_qv,
        d_w_out,
        d_b_out,
        d_gain_one,
        d_shift_one,
        d_w_up,
        d_b_up,
        d_w_down,
        d_b_down,
        d_gain_two,
        d_shift_two,
    )


def solution(mesh):
    placed = (
        P("docs", None),
        P("docs", None),
        P("docs"),
        P(None, None, "heads"),
        P(None, "heads"),
        P("heads", None),
        P(),
        P(),
        P(),
        P(None, "heads"),
        P("heads"),
        P("heads", None),
        P(),
        P(),
        P(),
    )
    return jax.shard_map(
        functools.partial(shards, mesh.shape["docs"]),
        mesh=mesh,
        in_specs=placed,
        out_specs=(
            P("docs", None),
            P("docs", None),
            P("docs", None, "heads"),
            P(None, "heads"),
            P("heads", "docs"),
            P(),
            P(),
            P(),
            P("docs", "heads"),
            P("heads"),
            P("heads", "docs"),
            P(),
            P(),
            P(),
        ),
        check_vma=False,
    )
```

```python
import functools

import jax
import jax.numpy as jnp
from jax import lax
from jax.experimental import pallas as pl
from jax.experimental.pallas import tpu as pltpu
from jax.sharding import PartitionSpec as P

HEAD_DIM = 64
SEG = 128
EPS = 1e-05
LANES = 128
F32 = jnp.float32
LOW = jnp.bfloat16
OWN = jnp.bfloat16
FF_CHUNK = 768
BLOCK = 256
VMEM_LIMIT = 60 * 1024 * 1024


def mm(first, second):
    return jnp.dot(first, second, preferred_element_type=F32)


def mm_nt(first, second):
    return lax.dot_general(first, second, (((1,), (1,)), ((), ())), preferred_element_type=F32)


def mm_tn(first, second):
    return lax.dot_general(first, second, (((0,), (0,)), ((), ())), preferred_element_type=F32)


def fold_rows(values):
    rows, width = values.shape
    return jnp.sum(values.reshape(rows // 8, 8, width), 0)


def gelu_pair(pre):
    below = 0.5 + 0.5 * lax.erf(pre * 0.7071067811865476)
    bell = jnp.exp2(pre * pre * (-0.5 * 1.4426950408889634))
    return pre * below, below + pre * bell * 0.3989422804014327


def const_spec(shape):
    zeros = (0,) * len(shape)
    return pl.BlockSpec(shape, lambda i, s: zeros, pipeline_mode=pl.Buffered(1))


def row_spec(block, width):
    return pl.BlockSpec((block, width), lambda i, s: (i, 0))


def cost(micros):
    return pl.CostEstimate(flops=0, bytes_accessed=int(micros * 3.69e6), transcendentals=0)


def params():
    return pltpu.CompilerParams(dimension_semantics=("arbitrary",), vmem_limit_bytes=VMEM_LIMIT)


def slots_of(width, parts):
    share = width // parts
    return (parts, share) if share % 16 == 0 else (1, width)


def arrange(grad, table, parts):
    if grad.shape[0] == parts:
        return grad
    spots = jnp.zeros((parts,), jnp.int32).at[table].set(jnp.arange(parts, dtype=jnp.int32))
    return jnp.take(grad.reshape(parts, -1, grad.shape[2]), spots, axis=0)


class Fetch:
    def __init__(self, sources, targets, sems):
        self.copies = [pltpu.make_async_copy(s, t, sems.at[i]) for i, (s, t) in enumerate(zip(sources, targets))]

    def start(self):
        @pl.when(pl.program_id(0) == 0)
        def _():
            for copy in self.copies:
                copy.start()

    def wait(self, *which):
        @pl.when(pl.program_id(0) == 0)
        def _():
            for i in which:
                self.copies[i].wait()


def fixed(shape):
    return pl.BlockSpec(shape, lambda i, s: (0,) * len(shape))


def spread(grad, out_ref, lanes, table, parts):
    if out_ref.shape[0] == 1:
        out_ref[0, :, lanes] = grad
        return
    share = grad.shape[0] // parts
    for part in range(parts):
        out_ref[table(part), :, lanes] = grad[part * share : (part + 1) * share]


def table_of(s_ref, kind, side, parts):
    return lambda part: s_ref[2 + (2 * kind + side) * parts + part]


def split_heads(values, masks):
    return jnp.concatenate([values * masks[0], values * masks[1]], 0)


def head_masks():
    left = lax.broadcasted_iota(jnp.int32, (SEG, LANES), 1) < HEAD_DIM
    return jnp.where(left, 1.0, 0.0).astype(LOW), jnp.where(left, 0.0, 1.0).astype(LOW)


ALL = slice(None)
ANY = pl.BlockSpec(memory_space=pl.ANY)


def row_of(ref):
    return ref[...].reshape(1, ref.shape[0])


def attn_fwd_kernel(block, rows, s_ref, x_ref, bo_ref, bt_ref, wo_hbm, wt_hbm, qkv_ref, p_ref, a_ref, w_ref, sems):
    cols = wo_hbm.shape[2]
    width = 2 * cols
    step = pl.program_id(0)
    fetch = Fetch(
        [w.at[kind] for kind in range(3) for w in (wo_hbm, wt_hbm)],
        [w_ref.at[:, (2 * kind + side) * cols : (2 * kind + side + 1) * cols] for kind in range(3) for side in range(2)],
        sems,
    )
    fetch.start()
    fetch.wait(*range(6))
    linear = mm(x_ref[...], w_ref[...])
    bias_q, bias_v = (jnp.concatenate([bo_ref[i : i + 1, :], bt_ref[i : i + 1, :]], 1) for i in range(2))
    q = ((linear[:, :width] + bias_q) * (HEAD_DIM**-0.5)).astype(LOW)
    k = linear[:, width : 2 * width].astype(LOW)
    v = (linear[:, 2 * width :] + bias_v).astype(LOW)
    qkv_ref[:, :width] = q
    qkv_ref[:, width : 2 * width] = k
    qkv_ref[:, 2 * width :] = v
    masks = head_masks()
    first_slot = s_ref[0] * rows + step * block
    for seg in range(block // SEG):
        at = slice(seg * SEG, (seg + 1) * SEG)
        slots = lax.broadcasted_iota(jnp.int32, (SEG, 2 * SEG), 0) + (first_slot + seg * SEG)
        bias = jnp.where(slots < s_ref[1], 0.0, -30000.0)
        for pair in range(width // LANES):
            lanes = slice(pair * LANES, (pair + 1) * LANES)
            scores = mm_nt(k[at, lanes], split_heads(q[at, lanes], masks)) + bias
            grown = jnp.exp(scores - jnp.max(scores, 0, keepdims=True))
            probs = (grown * (1.0 / jnp.sum(grown, 0, keepdims=True))).astype(LOW)
            p_ref[at, 2 * pair * SEG : 2 * (pair + 1) * SEG] = probs
            stacked = jnp.concatenate([probs[:, :SEG], probs[:, SEG:]], 0)
            a_ref[at, lanes] = mm_tn(stacked, split_heads(v[at, lanes], masks)).astype(LOW)


def attn_fwd(scal, tokens, w, b, rows, block):
    cols = w[0].shape[2]
    width = tokens.shape[1]
    steps = rows // block
    outs = [6 * cols, 2 * cols // HEAD_DIM * SEG, 2 * cols]
    return pl.pallas_call(
        functools.partial(attn_fwd_kernel, block, rows),
        grid_spec=pltpu.PrefetchScalarGridSpec(
            num_scalar_prefetch=1,
            grid=(steps,),
            in_specs=[pl.BlockSpec((block, width), lambda i, s: (s[0] * steps + i, 0))]
            + [const_spec(b[0].shape)] * 2
            + [ANY, ANY],
            out_specs=[row_spec(block, w) for w in outs],
            scratch_shapes=[pltpu.VMEM((width, 6 * cols), LOW), pltpu.SemaphoreType.DMA((6,))],
        ),
        out_shape=[jax.ShapeDtypeStruct((rows, w), LOW) for w in outs],
        compiler_params=params(),
        cost_estimate=cost(14),
        name="attn_fwd",
    )(scal, tokens, *b, *w)


def ffn_spots(half, chunk):
    return [
        (slice(side * half + start, side * half + start + chunk), side, slice(start, start + chunk))
        for side in range(2)
        for start in range(0, half, chunk)
    ]


def ffn_fwd_kernel(
    block, rows, chunk, parts, steps,
    s_ref, x_ref, g_ref, att_ref, bo_ref, bt_ref, bout_ref, g1_ref, h1_ref, bdown_ref, g2_ref, h2_ref,
    woo_hbm, wot_hbm, wuo_hbm, wut_hbm, wdo_hbm, wdt_hbm,
    out_ref, own_ref, gp_ref, low_ref, hat_ref, rs_ref, dmlp_ref, sums_ref, dt_ref, do_ref,
    wo_ref, wu_ref, wd_ref, sems, hid_ref, all_ref,
):
    step = pl.program_id(0)
    half = wuo_hbm.shape[1]
    cols = woo_hbm.shape[0]
    spots = ffn_spots(half, chunk)
    sources, targets = [woo_hbm, wot_hbm], [wo_ref.at[:cols], wo_ref.at[cols:]]
    for spot, side, local in spots:
        sources += [(wuo_hbm, wut_hbm)[side].at[:, local], (wdo_hbm, wdt_hbm)[side].at[local]]
        targets += [wu_ref.at[:, spot], wd_ref.at[spot]]
    fetch = Fetch(sources, targets, sems)
    fetch.start()

    @pl.when(step == 0)
    def _():
        sums_ref[...] = jnp.zeros_like(sums_ref)

    @pl.when(step < steps)
    def _():
        fetch.wait(0, 1)
        mine = pl.ds(pl.multiple_of(step * block, block), block)
        h1 = x_ref[...].astype(F32) + mm(att_ref[...], wo_ref[...]) + row_of(bout_ref)
        center = h1 - jnp.mean(h1, -1, keepdims=True)
        scale = lax.rsqrt(jnp.mean(center * center, -1, keepdims=True) + EPS)
        hat = center * scale
        hat_ref[...] = hat.astype(LOW)
        rs_ref[...] = jnp.broadcast_to(scale, rs_ref.shape)
        normed = hat * row_of(g1_ref) + row_of(h1_ref)
        low = normed.astype(LOW)
        low_ref[...] = low
        total = normed + row_of(bdown_ref)
        for i, (spot, side, local) in enumerate(spots):
            fetch.wait(2 + 2 * i, 3 + 2 * i)
            bias = (bo_ref, bt_ref)[side][pl.ds(local.start, chunk)].reshape(1, chunk)
            hidden, slope = gelu_pair(mm(low, wu_ref[:, spot]) + bias)
            hidden = hidden.astype(LOW)
            hid_ref[mine, spot] = hidden
            gp_ref[:, spot] = slope.astype(LOW)
            total = total + mm(hidden, wd_ref[spot, :])
        center = total - jnp.mean(total, -1, keepdims=True)
        scale = lax.rsqrt(jnp.mean(center * center, -1, keepdims=True) + EPS)
        hat = center * scale
        gain_two = row_of(g2_ref)
        result = (hat * gain_two + row_of(h2_ref)).astype(OWN)
        out_ref[...] = result.astype(F32)
        own_ref[...] = result
        slots = lax.broadcasted_iota(jnp.int32, (block, 1), 0) + (s_ref[0] * rows + step * block)
        cot = jnp.where(slots < s_ref[1], g_ref[...], 0.0)
        inner = cot * gain_two
        d_h2 = scale * (
            inner - jnp.mean(inner, -1, keepdims=True) - hat * jnp.mean(inner * hat, -1, keepdims=True)
        )
        d_mlp = d_h2.astype(LOW)
        dmlp_ref[...] = d_mlp
        all_ref[mine, :] = d_mlp
        sums_ref[0:8, :] += fold_rows(cot * hat)
        sums_ref[8:16, :] += fold_rows(cot)
        sums_ref[16:24, :] += fold_rows(d_h2)

    wide = dt_ref.shape[2]
    at = steps
    for side in (1, 0):
        for start in range(side * half, (side + 1) * half, wide):

            @pl.when(step == at)
            def _():
                grad = mm_tn(all_ref[...], hid_ref[:, start : start + wide]).astype(LOW)
                spread(grad, (do_ref, dt_ref)[side], ALL, table_of(s_ref, 0, side, parts), parts)

            at += 1


def ffn_fwd(scal, tokens, grad_out, att, w_out, w_up, b_up, w_down, vec, rows, block, chunk, wide, parts):
    width = tokens.shape[1]
    steps = rows // block
    half = w_up[0].shape[1]
    pieces = half // wide
    row = lambda i: jnp.minimum(i, steps - 1)
    mine = lambda i, s: (s[0] * steps + row(i), 0)
    rows_of = lambda w: pl.BlockSpec((block, w), lambda i, s: (row(i), 0))
    lead = slots_of(width, parts)
    weights = [*w_out, *w_up, *w_down]
    small = [*b_up, *vec]
    outs = [(width, OWN), (2 * half, LOW), (width, LOW), (width, LOW), (LANES, F32), (width, LOW)]
    piece_at = lambda k: pl.BlockSpec((*lead, wide), lambda i, s: (0, 0, jnp.clip(i - steps - k * pieces, 0, pieces - 1)))
    return pl.pallas_call(
        functools.partial(ffn_fwd_kernel, block, rows, chunk, parts, steps),
        grid_spec=pltpu.PrefetchScalarGridSpec(
            num_scalar_prefetch=1,
            grid=(steps + 2 * pieces,),
            in_specs=[pl.BlockSpec((block, width), mine), pl.BlockSpec((block, width), mine), rows_of(att.shape[1])]
            + [const_spec(v.shape) for v in small]
            + [ANY] * 6,
            out_specs=[pl.BlockSpec((block, width), mine)]
            + [rows_of(w) for w, _ in outs]
            + [fixed((24, width)), piece_at(0), piece_at(1)],
            scratch_shapes=[
                pltpu.VMEM((att.shape[1], width), LOW),
                pltpu.VMEM((width, 2 * half), LOW),
                pltpu.VMEM((2 * half, width), LOW),
                pltpu.SemaphoreType.DMA((2 + 4 * half // chunk,)),
                pltpu.VMEM((rows, 2 * half), LOW),
                pltpu.VMEM((rows, width), LOW),
            ],
        ),
        out_shape=[jax.ShapeDtypeStruct((2 * rows, width), F32)]
        + [jax.ShapeDtypeStruct((rows, w), t) for w, t in outs]
        + [jax.ShapeDtypeStruct((24, width), F32)]
        + [jax.ShapeDtypeStruct((*lead, half), LOW)] * 2,
        compiler_params=params(),
        cost_estimate=cost(35),
        name="ffn_fwd",
    )(scal, tokens, grad_out, att, *small, *weights)


def ffn_bwd_kernel(
    block, chunk, parts, steps,
    s_ref, dmlp_ref, gp_ref, hat_ref, rs_ref, g1_ref, woo_hbm, wot_hbm, wuo_hbm, wut_hbm, wdo_hbm, wdt_hbm, low_hbm, att_hbm,
    dh1_ref, datt_ref, sums_ref, bup_ref, ut_ref, uo_ref, ot_ref, oo_ref,
    wo_ref, wu_ref, wd_ref, low_ref, att_ref, sems, dpre_ref, dbr_ref,
):
    step = pl.program_id(0)
    half = wuo_hbm.shape[1]
    cols = woo_hbm.shape[0]
    spots = ffn_spots(half, chunk)
    sources, targets = [], []
    for spot, side, local in spots:
        sources += [(wdo_hbm, wdt_hbm)[side].at[local], (wuo_hbm, wut_hbm)[side].at[:, local]]
        targets += [wd_ref.at[spot], wu_ref.at[:, spot]]
    tail = len(sources)
    sources += [woo_hbm, wot_hbm, low_hbm, att_hbm]
    targets += [wo_ref.at[:cols], wo_ref.at[cols:], low_ref, att_ref]
    fetch = Fetch(sources, targets, sems)
    fetch.start()

    @pl.when(step == 0)
    def _():
        sums_ref[...] = jnp.zeros_like(sums_ref)
        bup_ref[...] = jnp.zeros_like(bup_ref)

    @pl.when(step < steps)
    def _():
        mine = pl.ds(pl.multiple_of(step * block, block), block)
        d_mlp = dmlp_ref[...]
        total = d_mlp.astype(F32)
        for i, (spot, side, local) in enumerate(spots):
            fetch.wait(2 * i, 2 * i + 1)
            d_pre = (mm_nt(d_mlp, wd_ref[spot, :]) * gp_ref[:, spot].astype(F32)).astype(LOW)
            dpre_ref[mine, spot] = d_pre
            bup_ref[:, spot] += fold_rows(d_pre.astype(F32))
            total = total + mm_nt(d_pre, wu_ref[:, spot])
        hat = hat_ref[...].astype(F32)
        inner = total * row_of(g1_ref)
        d_h1 = rs_ref[:, 0:1] * (
            inner - jnp.mean(inner, -1, keepdims=True) - hat * jnp.mean(inner * hat, -1, keepdims=True)
        )
        sums_ref[0:8, :] += fold_rows(total * hat)
        sums_ref[8:16, :] += fold_rows(total)
        sums_ref[16:24, :] += fold_rows(d_h1)
        dh1_ref[...] = d_h1
        low = d_h1.astype(LOW)
        dbr_ref[mine, :] = low
        fetch.wait(tail, tail + 1)
        datt_ref[...] = mm_nt(low, wo_ref[...]).astype(LOW)

    @pl.when(step == steps - 1)
    def _():
        for i in (tail + 2, tail + 3):
            fetch.copies[i].wait()

    wide = ut_ref.shape[2]
    at = steps
    for side in (1, 0):
        for start in range(side * half, (side + 1) * half, wide):

            @pl.when(step == at)
            def _():
                grad = mm_tn(low_ref[...], dpre_ref[:, start : start + wide]).astype(LOW)
                spread(grad, (uo_ref, ut_ref)[side], ALL, table_of(s_ref, 1, side, parts), parts)

            at += 1

    @pl.when(step == at)
    def _():
        grad = mm_tn(dbr_ref[...], att_ref[...]).astype(LOW)
        spread(grad[:, :cols], oo_ref, ALL, table_of(s_ref, 1, 0, parts), parts)
        spread(grad[:, cols:], ot_ref, ALL, table_of(s_ref, 1, 1, parts), parts)


def ffn_bwd(scal, d_mlp, slope, hat, scale, normed_low, att, w_out, w_up, w_down, gain_one, block, chunk, wide, parts):
    rows, width = d_mlp.shape
    steps = rows // block
    half = w_up[0].shape[1]
    pieces = half // wide
    cols = w_out[0].shape[0]
    rows_of = lambda w: pl.BlockSpec((block, w), lambda i, s: (jnp.minimum(i, steps - 1), 0))
    moving = [d_mlp, slope, hat, scale]
    lead = slots_of(width, parts)
    piece_at = lambda k: pl.BlockSpec((*lead, wide), lambda i, s: (0, 0, jnp.clip(i - steps - k * pieces, 0, pieces - 1)))
    return pl.pallas_call(
        functools.partial(ffn_bwd_kernel, block, chunk, parts, steps),
        grid_spec=pltpu.PrefetchScalarGridSpec(
            num_scalar_prefetch=1,
            grid=(steps + 2 * pieces + 1,),
            in_specs=[rows_of(m.shape[1]) for m in moving] + [const_spec(gain_one.shape)] + [ANY] * 8,
            out_specs=[rows_of(width), rows_of(2 * cols), fixed((24, width)), fixed((8, 2 * half))]
            + [piece_at(0), piece_at(1)]
            + [fixed((*lead, cols))] * 2,
            scratch_shapes=[
                pltpu.VMEM((2 * cols, width), LOW),
                pltpu.VMEM((width, 2 * half), LOW),
                pltpu.VMEM((2 * half, width), LOW),
                pltpu.VMEM((rows, width), LOW),
                pltpu.VMEM((rows, 2 * cols), LOW),
                pltpu.SemaphoreType.DMA((4 + 4 * half // chunk,)),
                pltpu.VMEM((rows, 2 * half), LOW),
                pltpu.VMEM((rows, width), LOW),
            ],
        ),
        out_shape=[
            jax.ShapeDtypeStruct((rows, width), F32),
            jax.ShapeDtypeStruct((rows, 2 * cols), LOW),
            jax.ShapeDtypeStruct((24, width), F32),
            jax.ShapeDtypeStruct((8, 2 * half), F32),
        ]
        + [jax.ShapeDtypeStruct((*lead, half), LOW)] * 2
        + [jax.ShapeDtypeStruct((*lead, cols), LOW)] * 2,
        compiler_params=params(),
        cost_estimate=cost(32),
        name="ffn_bwd",
    )(scal, *moving, gain_one, *w_out, *w_up, *w_down, normed_low, att)


def attn_bwd_kernel(block, side, parts, steps, s_ref, *refs):
    q_ref, k_ref, v_ref, p_ref, da_ref, base_ref, x_hbm, w_hbm = refs[:8]
    if side:
        part_ref, _, sum_ref, grad_ref, tok_ref, whole_ref = refs[8:-5]
    else:
        two_ref, one_ref, bup_ref, other_ref, sum_ref, grad_ref, tok_ref, own_ref, keep_ref, send_ref = refs[8:-5]
    x_ref, w_ref, sems, all_ref, dl_ref = refs[-5:]
    step = pl.program_id(0)
    cols = da_ref.shape[1]
    rows = x_ref.shape[0]
    fetch = Fetch(
        [w_hbm.at[kind] for kind in range(3)] + [x_hbm.at[pl.ds(pl.multiple_of(s_ref[0] * rows, rows), rows)]],
        [w_ref.at[:, kind * cols : (kind + 1) * cols] for kind in range(3)] + [x_ref],
        sems,
    )
    fetch.start()

    @pl.when(step == 0)
    def _():
        sum_ref[...] = jnp.zeros_like(sum_ref)

    @pl.when(step < steps)
    def _():
        if side:
            whole_ref[...] = part_ref[...].astype(whole_ref.dtype)
        masks = head_masks()
        for seg in range(block // SEG):
            at = slice(seg * SEG, (seg + 1) * SEG)
            for pair in range(cols // LANES):
                lanes = slice(pair * LANES, (pair + 1) * LANES)
                k_lanes = slice(cols + pair * LANES, cols + (pair + 1) * LANES)
                v_lanes = slice(2 * cols + pair * LANES, 2 * cols + (pair + 1) * LANES)
                low_probs = p_ref[at, 2 * pair * SEG : 2 * (pair + 1) * SEG]
                probs = low_probs.astype(F32)
                d_att = split_heads(da_ref[at, lanes], masks)
                d_probs = mm_nt(v_ref[at, lanes], d_att)
                d_scores = (probs * (d_probs - jnp.sum(probs * d_probs, 0, keepdims=True))).astype(LOW)
                d_v = mm(low_probs, d_att).astype(LOW)
                d_k = mm(d_scores, split_heads(q_ref[at, lanes], masks)).astype(LOW)
                stacked = jnp.concatenate([d_scores[:, :SEG], d_scores[:, SEG:]], 0)
                d_q = (mm_tn(stacked, split_heads(k_ref[at, lanes], masks)) * (HEAD_DIM**-0.5)).astype(LOW)
                dl_ref[at, lanes] = d_q
                dl_ref[at, k_lanes] = d_k
                dl_ref[at, v_lanes] = d_v
                sum_ref[:, lanes] += fold_rows(d_q.astype(F32))
                sum_ref[:, k_lanes] += fold_rows(d_v.astype(F32))
        all_ref[pl.ds(pl.multiple_of(step * block, block), block), :] = dl_ref[...]
        fetch.wait(0, 1, 2)
        total = base_ref[...] + mm_nt(dl_ref[...], w_ref[...])
        if side:
            tok_ref[...] = total
        else:
            total = total.astype(OWN)
            tok_ref[...] = total.astype(F32)
            own_ref[...] = total

    @pl.when(step == steps)
    def _():
        fetch.copies[3].wait()
        grad = mm_tn(x_ref[...], all_ref[...]).astype(LOW)
        spread(grad, grad_ref, ALL, table_of(s_ref, 0, side, parts), parts)
        if not side:
            half = bup_ref.shape[1] // 2
            width = one_ref.shape[1]
            for to, ref, sum_of in ((0, keep_ref, sum_ref), (1, send_ref, other_ref)):
                ref[...] = jnp.zeros_like(ref)
                at = 0
                pieces = [(norm, 8 * group, 0, width) for norm in (two_ref, one_ref) for group in range(3)]
                pieces += [(bup_ref, 0, to * half, half), (sum_of, 0, 0, 2 * cols)]
                for source, top, start, count in pieces:
                    total = jnp.sum(source[top : top + 8, start : start + count], 0, keepdims=True)
                    for piece in range(count // LANES):
                        ref[at : at + 1, :] = total[:, piece * LANES : (piece + 1) * LANES]
                        at += 1


def attn_bwd(scal, qkv, probs, d_att, base, w, extra, tokens, side, block, parts):
    rows = qkv.shape[0]
    width = tokens.shape[1]
    cols = d_att.shape[1] // 2
    steps = rows // block
    row = lambda i: jnp.minimum(i, steps - 1)
    part_of = lambda w, at: pl.BlockSpec((block, w), lambda i, s: (row(i), at))
    lead = slots_of(width, parts)
    in_specs = [part_of(cols, 2 * kind + side) for kind in range(3)] + [part_of(probs.shape[1] // 2, side), part_of(cols, side)]
    in_specs += [part_of(width, 0), ANY, ANY]
    out_specs = [fixed((8, 2 * cols)), fixed((*lead, 3 * cols))]
    out_shape = [jax.ShapeDtypeStruct((8, 2 * cols), F32), jax.ShapeDtypeStruct((*lead, 3 * cols), LOW)]
    if side:
        in_specs += [part_of(width, 0), ANY]
        out_specs += [part_of(width, 0), pl.BlockSpec((block, width), lambda i, s: ((1 - s[0]) * steps + row(i), 0))]
        out_shape += [jax.ShapeDtypeStruct((rows, width), F32), jax.ShapeDtypeStruct(extra[1].shape, F32)]
    else:
        in_specs += [const_spec(m.shape) for m in extra]
        small = -(-(6 * width + extra[2].shape[1] // 2 + 2 * cols) // (8 * LANES)) * 8
        out_specs += [pl.BlockSpec((block, width), lambda i, s: (s[0] * steps + row(i), 0)), part_of(width, 0)]
        out_specs += [fixed((small, LANES))] * 2
        out_shape += [jax.ShapeDtypeStruct((2 * rows, width), F32), jax.ShapeDtypeStruct((rows, width), OWN)]
        out_shape += [jax.ShapeDtypeStruct((small, LANES), F32)] * 2
    return pl.pallas_call(
        functools.partial(attn_bwd_kernel, block, side, parts, steps),
        grid_spec=pltpu.PrefetchScalarGridSpec(
            num_scalar_prefetch=1,
            grid=(steps + 1,),
            in_specs=in_specs,
            out_specs=out_specs,
            scratch_shapes=[
                pltpu.VMEM((rows, width), LOW),
                pltpu.VMEM((width, 3 * cols), LOW),
                pltpu.SemaphoreType.DMA((4,)),
                pltpu.VMEM((rows, 3 * cols), LOW),
                pltpu.VMEM((block, 3 * cols), LOW),
            ],
        ),
        out_shape=out_shape,
        input_output_aliases={10: 3} if side else {},
        compiler_params=params(),
        cost_estimate=cost(15),
        name="attn_bwd",
    )(scal, qkv, qkv, qkv, probs, d_att, base, tokens, w, *extra)


def place_kernel(s_ref, whole_ref, part_ref, out_ref):
    out_ref[...] = part_ref[...].astype(out_ref.dtype)


def place_other(scal, whole, piece, block):
    rows, width = piece.shape
    steps = rows // block
    return pl.pallas_call(
        place_kernel,
        grid_spec=pltpu.PrefetchScalarGridSpec(
            num_scalar_prefetch=1,
            grid=(steps,),
            in_specs=[ANY, row_spec(block, width)],
            out_specs=pl.BlockSpec((block, width), lambda i, s: ((1 - s[0]) * steps + i, 0)),
        ),
        out_shape=jax.ShapeDtypeStruct(whole.shape, F32),
        input_output_aliases={1: 0},
        compiler_params=params(),
        cost_estimate=cost(4),
        name="place_other",
    )(scal, whole, piece)


def shards(
    n_docs, tokens, grad_out, live_tokens, w_qkv, b_qv, w_out, b_out, gain_one, shift_one, w_up, b_up, w_down, b_down,
    gain_two, shift_two,
):
    c = lax.axis_index("heads")
    me = lax.axis_index("docs")
    rows = tokens.shape[0] // 2
    bits = n_docs.bit_length() - 1
    rest = list(range(2, bits))
    orders = [[[0, 1, *rest], [1, 0, *rest]]] * 2

    def step(value, kind, stage):
        pairs = [(d * 2 + h, (d ^ (1 << orders[kind][h][stage])) * 2 + h) for d in range(n_docs) for h in range(2)]
        return lax.ppermute(value, ("docs", "heads"), pairs)

    def swap(value):
        return lax.ppermute(value, "heads", [(0, 1), (1, 0)])

    def after(value, *before):
        return lax.optimization_barrier((value, *before))[0]

    def table_for(kind, core):
        away = jnp.arange(n_docs, dtype=jnp.int32) ^ me
        slots = []
        for order in orders[kind]:
            slot = jnp.zeros((n_docs,), jnp.int32)
            for place, bit in enumerate(order):
                slot = slot | (((away >> bit) & 1) << (bits - 1 - place))
            slots.append(slot)
        return jnp.where(core == 0, slots[0], slots[1])

    tables = [table_for(kind, core) for kind in range(2) for core in (c, 1 - c)]
    scal = jnp.concatenate([c[None].astype(jnp.int32), live_tokens, *tables])

    w_qkv = jnp.transpose(w_qkv, (1, 0, 2))
    w_qkv2 = (w_qkv, swap(w_qkv))
    b_qv2 = (b_qv, swap(b_qv))
    b_up2 = (b_up, swap(b_up))
    w_out, w_up, w_down = after((w_out, w_up, w_down), w_qkv2[1], b_qv2[1], b_up2[1])
    w_out2 = (w_out, swap(w_out))
    w_up2 = (w_up, swap(w_up))
    w_down2 = (w_down, swap(w_down))
    vec = (b_out, gain_one, shift_one, b_down, gain_two, shift_two)

    def add(left, right):
        return (left.astype(F32) + right.astype(F32)).astype(LOW)

    def first_sum(kind, pairs):
        half = n_docs // 2
        parts = [(arrange(own, tables[2 * kind], n_docs), arrange(swap(other), tables[2 * kind], n_docs)) for own, other in pairs]
        cut = lambda at: jnp.concatenate([add(own[at], other[at]) for own, other in parts], 2)
        return cut(slice(half, None)), cut(slice(None, half))

    def next_sum(keep, came):
        half = keep.shape[0] // 2
        if not half:
            return (keep.astype(F32) + came.astype(F32))[0]
        return add(keep[half:], came[half:]), add(keep[:half], came[:half])

    half = w_up.shape[1]
    cols = w_out.shape[0]
    qkv, probs, att = attn_fwd(scal, tokens, w_qkv2, b_qv2, rows, BLOCK)
    def stage_of(kind, pair, stage, *before):
        return next_sum(after(pair[1], *before), step(pair[0], kind, stage))

    layer_out, layer_own, slope, normed_low, hat, scale, d_mlp, sums_two, down_other, down_own = ffn_fwd(
        scal, tokens, grad_out, att, w_out2, w_up2, b_up2, w_down2, vec, rows, BLOCK, FF_CHUNK, 768, n_docs
    )
    down = first_sum(0, [(down_own, down_other)])
    d_mlp = after(d_mlp, down[0])
    d_h1, d_att, sums_one, sums_up, up_other, up_own, out_other, out_own = ffn_bwd(
        scal, d_mlp, slope, hat, scale, normed_low, att, w_out2, w_up2, w_down2, gain_one, BLOCK, FF_CHUNK, 768, n_docs
    )
    down = stage_of(0, down, 0, up_own)
    up_own, up_other, out_own, out_other, layer_own = after((up_own, up_other, out_own, out_other, layer_own), down[0])
    up = first_sum(1, [(up_own, up_other), (out_own, out_other)])
    sums_other, qkv_other, d_tokens, layer_out = attn_bwd(
        scal, qkv, probs, after(d_att, *up), d_h1, w_qkv2[1], (swap(layer_own), layer_out), tokens, 1, BLOCK, n_docs
    )
    down = stage_of(0, down, 1, qkv_other)
    qkv_other, keep_up = after((qkv_other, up[1]), down[0])
    up = stage_of(1, (up[0], keep_up), 0)
    sums = (sums_two, sums_one, sums_up, sums_other)
    _, qkv_own, d_tokens, tokens_own, small_keep, small_send = attn_bwd(
        scal, qkv, probs, after(d_att, up[0]), d_tokens, w_qkv2[0], sums, tokens, 0, BLOCK, n_docs
    )

    def spread_small(small, stage, *before):
        pairs = [(d, d ^ (1 << stage)) for d in range(n_docs)]
        return after(small, *before) + lax.ppermute(small, "docs", pairs)

    down = stage_of(0, down, 2, qkv_own)
    lin = first_sum(0, [(after(qkv_own, down[0]), qkv_other)])
    up = stage_of(1, up, 1, lin[0])
    small = after(small_keep, up[0]) + swap(after(small_send, down[0]))
    lin = stage_of(0, lin, 0, small)
    d_tokens = place_other(scal, after(d_tokens, lin[0]), swap(after(tokens_own, down[0])), 2 * BLOCK)
    small = spread_small(small, 0, d_tokens)
    up = stage_of(1, up, 2, small)
    last = up[0]
    for stage in range(1, bits - 1):
        lin = stage_of(0, lin, stage, last)
        if stage + 2 < bits:
            down = stage_of(0, down, stage + 2, lin[0])
        if stage + 3 < bits:
            up = stage_of(1, up, stage + 2, down[0])
        if stage == bits - 2:
            up = stage_of(1, up, bits - 1, lin[0])
        small = spread_small(small, stage, up[0], down[0])
        last = small
    small = spread_small(small, bits - 1, up)
    lin = stage_of(0, lin, bits - 1, small)
    d_w_down = down.T
    d_w_up, d_w_out = up[:, :half], up[:, half:].T
    d_w_qkv = lin.reshape(-1, 3, cols)
    small = small.reshape(-1)
    width = tokens.shape[1]
    d_gain_two, d_shift_two, d_b_down, d_gain_one, d_shift_one, d_b_out = (
        small[i * width : (i + 1) * width] for i in range(6)
    )
    d_b_up = small[6 * width : 6 * width + half]
    d_b_qv = small[6 * width + half : 7 * width + half].reshape(2, cols)
    return (
        layer_out,
        d_tokens,
        d_w_qkv,
        d_b_qv,
        d_w_out,
        d_b_out,
        d_gain_one,
        d_shift_one,
        d_w_up,
        d_b_up,
        d_w_down,
        d_b_down,
        d_gain_two,
        d_shift_two,
    )


def solution(mesh):
    placed = (
        P("docs", None),
        P("docs", None),
        P("docs"),
        P(None, None, "heads"),
        P(None, "heads"),
        P("heads", None),
        P(),
        P(),
        P(),
        P(None, "heads"),
        P("heads"),
        P("heads", None),
        P(),
        P(),
        P(),
    )
    return jax.shard_map(
        functools.partial(shards, mesh.shape["docs"]),
        mesh=mesh,
        in_specs=placed,
        out_specs=(
            P("docs", None),
            P("docs", None),
            P("docs", None, "heads"),
            P(None, "heads"),
            P("heads", "docs"),
            P(),
            P(),
            P(),
            P("docs", "heads"),
            P("heads"),
            P("heads", "docs"),
            P(),
            P(),
            P(),
        ),
        check_vma=False,
    )
```

```python
import functools

import jax
import jax.numpy as jnp
from jax import lax
from jax.experimental import pallas as pl
from jax.experimental.pallas import tpu as pltpu
from jax.sharding import PartitionSpec as P

HEAD_DIM = 64
SEG = 128
EPS = 1e-05
LANES = 128
F32 = jnp.float32
LOW = jnp.bfloat16
OWN = jnp.bfloat16
FF_CHUNK = 1536
BLOCK = 256
MIB = 1024 * 1024


def mm(first, second):
    return jnp.dot(first, second, preferred_element_type=F32)


def mm_nt(first, second):
    return lax.dot_general(first, second, (((1,), (1,)), ((), ())), preferred_element_type=F32)


def mm_tn(first, second):
    return lax.dot_general(first, second, (((0,), (0,)), ((), ())), preferred_element_type=F32)


def fold_rows(values):
    rows, width = values.shape
    return jnp.sum(values.reshape(rows // 8, 8, width), 0)


def gelu_pair(pre):
    below = 0.5 + 0.5 * lax.erf(pre * 0.7071067811865476)
    bell = jnp.exp2(pre * pre * (-0.5 * 1.4426950408889634))
    return pre * below, below + pre * bell * 0.3989422804014327


def const_spec(shape):
    zeros = (0,) * len(shape)
    return pl.BlockSpec(shape, lambda i, s: zeros, pipeline_mode=pl.Buffered(1))


def row_spec(block, width):
    return pl.BlockSpec((block, width), lambda i, s: (i, 0))


def cost(micros):
    return pl.CostEstimate(flops=0, bytes_accessed=int(micros * 3.69e6), transcendentals=0)


def params(mebibytes):
    return pltpu.CompilerParams(dimension_semantics=("arbitrary",), vmem_limit_bytes=mebibytes * MIB)


def slots_of(width, parts):
    share = width // parts
    return (parts, share) if share % 16 == 0 else (1, width)


def arrange(grad, table, parts):
    if grad.shape[0] == parts:
        return grad
    spots = jnp.zeros((parts,), jnp.int32).at[table].set(jnp.arange(parts, dtype=jnp.int32))
    return jnp.take(grad.reshape(parts, -1, grad.shape[2]), spots, axis=0)


class Fetch:
    def __init__(self, sources, targets, sems):
        self.copies = [pltpu.make_async_copy(s, t, sems.at[i]) for i, (s, t) in enumerate(zip(sources, targets))]

    def start(self):
        @pl.when(pl.program_id(0) == 0)
        def _():
            for copy in self.copies:
                copy.start()

    def wait(self, *which):
        @pl.when(pl.program_id(0) == 0)
        def _():
            for i in which:
                self.copies[i].wait()


def fixed(shape):
    return pl.BlockSpec(shape, lambda i, s: (0,) * len(shape))


def spread(grad, out_ref, lanes, table, parts):
    if out_ref.shape[0] == 1:
        out_ref[0, :, lanes] = grad
        return
    share = grad.shape[0] // parts
    for part in range(parts):
        out_ref[table(part), :, lanes] = grad[part * share : (part + 1) * share]


def table_of(s_ref, kind, side, parts):
    return lambda part: s_ref[2 + (2 * kind + side) * parts + part]


def split_heads(values, masks):
    return jnp.concatenate([values * masks[0], values * masks[1]], 0)


def head_masks():
    left = lax.broadcasted_iota(jnp.int32, (SEG, LANES), 1) < HEAD_DIM
    return jnp.where(left, 1.0, 0.0).astype(LOW), jnp.where(left, 0.0, 1.0).astype(LOW)


ALL = slice(None)
ANY = pl.BlockSpec(memory_space=pl.ANY)


def row_of(ref):
    return ref[...].reshape(1, ref.shape[0])


def attn_fwd_kernel(block, rows, s_ref, x_ref, bo_ref, bt_ref, wo_hbm, wt_hbm, qkv_ref, p_ref, a_ref, w_ref, sems):
    cols = wo_hbm.shape[2]
    width = 2 * cols
    step = pl.program_id(0)
    fetch = Fetch(
        [w.at[kind] for kind in range(3) for w in (wo_hbm, wt_hbm)],
        [w_ref.at[:, (2 * kind + side) * cols : (2 * kind + side + 1) * cols] for kind in range(3) for side in range(2)],
        sems,
    )
    fetch.start()
    fetch.wait(*range(6))
    linear = mm(x_ref[...], w_ref[...])
    bias_q, bias_v = (jnp.concatenate([bo_ref[i : i + 1, :], bt_ref[i : i + 1, :]], 1) for i in range(2))
    q = ((linear[:, :width] + bias_q) * (HEAD_DIM**-0.5)).astype(LOW)
    k = linear[:, width : 2 * width].astype(LOW)
    v = (linear[:, 2 * width :] + bias_v).astype(LOW)
    qkv_ref[:, :width] = q
    qkv_ref[:, width : 2 * width] = k
    qkv_ref[:, 2 * width :] = v
    masks = head_masks()
    first_slot = s_ref[0] * rows + step * block
    for seg in range(block // SEG):
        at = slice(seg * SEG, (seg + 1) * SEG)
        slots = lax.broadcasted_iota(jnp.int32, (SEG, 2 * SEG), 0) + (first_slot + seg * SEG)
        bias = jnp.where(slots < s_ref[1], 0.0, -30000.0)
        for pair in range(width // LANES):
            lanes = slice(pair * LANES, (pair + 1) * LANES)
            scores = mm_nt(k[at, lanes], split_heads(q[at, lanes], masks)) + bias
            grown = jnp.exp(scores - jnp.max(scores, 0, keepdims=True))
            probs = (grown * (1.0 / jnp.sum(grown, 0, keepdims=True))).astype(LOW)
            p_ref[at, 2 * pair * SEG : 2 * (pair + 1) * SEG] = probs
            stacked = jnp.concatenate([probs[:, :SEG], probs[:, SEG:]], 0)
            a_ref[at, lanes] = mm_tn(stacked, split_heads(v[at, lanes], masks)).astype(LOW)


def attn_fwd(scal, tokens, w, b, rows, block):
    cols = w[0].shape[2]
    width = tokens.shape[1]
    steps = rows // block
    outs = [6 * cols, 2 * cols // HEAD_DIM * SEG, 2 * cols]
    return pl.pallas_call(
        functools.partial(attn_fwd_kernel, block, rows),
        grid_spec=pltpu.PrefetchScalarGridSpec(
            num_scalar_prefetch=1,
            grid=(steps,),
            in_specs=[pl.BlockSpec((block, width), lambda i, s: (s[0] * steps + i, 0))]
            + [const_spec(b[0].shape)] * 2
            + [ANY, ANY],
            out_specs=[row_spec(block, w) for w in outs],
            scratch_shapes=[pltpu.VMEM((width, 6 * cols), LOW), pltpu.SemaphoreType.DMA((6,))],
        ),
        out_shape=[jax.ShapeDtypeStruct((rows, w), LOW) for w in outs],
        compiler_params=params(60),
        cost_estimate=cost(14),
        name="attn_fwd",
    )(scal, tokens, *b, *w)


def ffn_spots(half, chunk):
    return [
        (slice(side * half + start, side * half + start + chunk), side, slice(start, start + chunk))
        for side in range(2)
        for start in range(0, half, chunk)
    ]


def ffn_fwd_kernel(
    block, rows, chunk, parts, steps,
    s_ref, x_ref, g_ref, att_ref, bo_ref, bt_ref, bout_ref, g1_ref, h1_ref, bdown_ref, g2_ref, h2_ref,
    woo_hbm, wot_hbm, wuo_hbm, wut_hbm, wdo_hbm, wdt_hbm,
    out_ref, own_ref, gp_ref, low_ref, hat_ref, rs_ref, dmlp_ref, sums_ref, dt_ref, do_ref,
    wo_ref, wu_ref, wd_ref, sems, hid_ref, all_ref,
):
    step = pl.program_id(0)
    half = wuo_hbm.shape[1]
    cols = woo_hbm.shape[0]
    spots = ffn_spots(half, chunk)
    sources, targets = [woo_hbm, wot_hbm], [wo_ref.at[:cols], wo_ref.at[cols:]]
    for spot, side, local in spots:
        sources += [(wuo_hbm, wut_hbm)[side].at[:, local], (wdo_hbm, wdt_hbm)[side].at[local]]
        targets += [wu_ref.at[:, spot], wd_ref.at[spot]]
    fetch = Fetch(sources, targets, sems)
    fetch.start()

    @pl.when(step == 0)
    def _():
        sums_ref[...] = jnp.zeros_like(sums_ref)

    @pl.when(step < steps)
    def _():
        fetch.wait(0, 1)
        mine = pl.ds(pl.multiple_of(step * block, block), block)
        h1 = x_ref[...].astype(F32) + mm(att_ref[...], wo_ref[...]) + row_of(bout_ref)
        center = h1 - jnp.mean(h1, -1, keepdims=True)
        scale = lax.rsqrt(jnp.mean(center * center, -1, keepdims=True) + EPS)
        hat = center * scale
        hat_ref[...] = hat.astype(LOW)
        rs_ref[...] = jnp.broadcast_to(scale, rs_ref.shape)
        normed = hat * row_of(g1_ref) + row_of(h1_ref)
        low = normed.astype(LOW)
        low_ref[...] = low
        total = normed + row_of(bdown_ref)
        for i, (spot, side, local) in enumerate(spots):
            fetch.wait(2 + 2 * i, 3 + 2 * i)
            bias = (bo_ref, bt_ref)[side][pl.ds(local.start, chunk)].reshape(1, chunk)
            hidden, slope = gelu_pair(mm(low, wu_ref[:, spot]) + bias)
            hidden = hidden.astype(LOW)
            hid_ref[mine, spot] = hidden
            gp_ref[:, spot] = slope.astype(LOW)
            total = total + mm(hidden, wd_ref[spot, :])
        center = total - jnp.mean(total, -1, keepdims=True)
        scale = lax.rsqrt(jnp.mean(center * center, -1, keepdims=True) + EPS)
        hat = center * scale
        gain_two = row_of(g2_ref)
        result = (hat * gain_two + row_of(h2_ref)).astype(OWN)
        out_ref[...] = result.astype(F32)
        own_ref[...] = result
        slots = lax.broadcasted_iota(jnp.int32, (block, 1), 0) + (s_ref[0] * rows + step * block)
        cot = jnp.where(slots < s_ref[1], g_ref[...], 0.0)
        inner = cot * gain_two
        d_h2 = scale * (
            inner - jnp.mean(inner, -1, keepdims=True) - hat * jnp.mean(inner * hat, -1, keepdims=True)
        )
        d_mlp = d_h2.astype(LOW)
        dmlp_ref[...] = d_mlp
        all_ref[mine, :] = d_mlp
        sums_ref[0:8, :] += fold_rows(cot * hat)
        sums_ref[8:16, :] += fold_rows(cot)
        sums_ref[16:24, :] += fold_rows(d_h2)

    wide = dt_ref.shape[2]
    at = steps
    for side in (1, 0):
        for start in range(side * half, (side + 1) * half, wide):

            @pl.when(step == at)
            def _():
                grad = mm_tn(all_ref[...], hid_ref[:, start : start + wide]).astype(LOW)
                spread(grad, (do_ref, dt_ref)[side], ALL, table_of(s_ref, 0, side, parts), parts)

            at += 1


def ffn_fwd(scal, tokens, grad_out, att, w_out, w_up, b_up, w_down, vec, rows, block, chunk, wide, parts):
    width = tokens.shape[1]
    steps = rows // block
    half = w_up[0].shape[1]
    pieces = half // wide
    row = lambda i: jnp.minimum(i, steps - 1)
    mine = lambda i, s: (s[0] * steps + row(i), 0)
    rows_of = lambda w: pl.BlockSpec((block, w), lambda i, s: (row(i), 0))
    lead = slots_of(width, parts)
    weights = [*w_out, *w_up, *w_down]
    small = [*b_up, *vec]
    outs = [(width, OWN), (2 * half, LOW), (width, LOW), (width, LOW), (LANES, F32), (width, LOW)]
    piece_at = lambda k: pl.BlockSpec((*lead, wide), lambda i, s: (0, 0, jnp.clip(i - steps - k * pieces, 0, pieces - 1)))
    return pl.pallas_call(
        functools.partial(ffn_fwd_kernel, block, rows, chunk, parts, steps),
        grid_spec=pltpu.PrefetchScalarGridSpec(
            num_scalar_prefetch=1,
            grid=(steps + 2 * pieces,),
            in_specs=[pl.BlockSpec((block, width), mine), pl.BlockSpec((block, width), mine), rows_of(att.shape[1])]
            + [const_spec(v.shape) for v in small]
            + [ANY] * 6,
            out_specs=[pl.BlockSpec((block, width), mine)]
            + [rows_of(w) for w, _ in outs]
            + [fixed((24, width)), piece_at(0), piece_at(1)],
            scratch_shapes=[
                pltpu.VMEM((att.shape[1], width), LOW),
                pltpu.VMEM((width, 2 * half), LOW),
                pltpu.VMEM((2 * half, width), LOW),
                pltpu.SemaphoreType.DMA((2 + 4 * half // chunk,)),
                pltpu.VMEM((rows, 2 * half), LOW),
                pltpu.VMEM((rows, width), LOW),
            ],
        ),
        out_shape=[jax.ShapeDtypeStruct((2 * rows, width), F32)]
        + [jax.ShapeDtypeStruct((rows, w), t) for w, t in outs]
        + [jax.ShapeDtypeStruct((24, width), F32)]
        + [jax.ShapeDtypeStruct((*lead, half), LOW)] * 2,
        compiler_params=params(50),
        cost_estimate=cost(35),
        name="ffn_fwd",
    )(scal, tokens, grad_out, att, *small, *weights)


def ffn_bwd_kernel(
    block, chunk, parts, steps,
    s_ref, dmlp_ref, gp_ref, hat_ref, rs_ref, g1_ref, woo_hbm, wot_hbm, wuo_hbm, wut_hbm, wdo_hbm, wdt_hbm, low_hbm, att_hbm,
    dh1_ref, datt_ref, sums_ref, bup_ref, ut_ref, uo_ref, ot_ref, oo_ref,
    wo_ref, wu_ref, wd_ref, low_ref, att_ref, sems, dpre_ref, dbr_ref,
):
    step = pl.program_id(0)
    half = wuo_hbm.shape[1]
    cols = woo_hbm.shape[0]
    spots = ffn_spots(half, chunk)
    sources, targets = [], []
    for spot, side, local in spots:
        sources += [(wdo_hbm, wdt_hbm)[side].at[local], (wuo_hbm, wut_hbm)[side].at[:, local]]
        targets += [wd_ref.at[spot], wu_ref.at[:, spot]]
    tail = len(sources)
    sources += [woo_hbm, wot_hbm, low_hbm, att_hbm]
    targets += [wo_ref.at[:cols], wo_ref.at[cols:], low_ref, att_ref]
    fetch = Fetch(sources, targets, sems)
    fetch.start()

    @pl.when(step == 0)
    def _():
        sums_ref[...] = jnp.zeros_like(sums_ref)
        bup_ref[...] = jnp.zeros_like(bup_ref)

    @pl.when(step < steps)
    def _():
        mine = pl.ds(pl.multiple_of(step * block, block), block)
        d_mlp = dmlp_ref[...]
        total = d_mlp.astype(F32)
        for i, (spot, side, local) in enumerate(spots):
            fetch.wait(2 * i, 2 * i + 1)
            d_pre = (mm_nt(d_mlp, wd_ref[spot, :]) * gp_ref[:, spot].astype(F32)).astype(LOW)
            dpre_ref[mine, spot] = d_pre
            bup_ref[:, spot] += fold_rows(d_pre.astype(F32))
            total = total + mm_nt(d_pre, wu_ref[:, spot])
        hat = hat_ref[...].astype(F32)
        inner = total * row_of(g1_ref)
        d_h1 = rs_ref[:, 0:1] * (
            inner - jnp.mean(inner, -1, keepdims=True) - hat * jnp.mean(inner * hat, -1, keepdims=True)
        )
        sums_ref[0:8, :] += fold_rows(total * hat)
        sums_ref[8:16, :] += fold_rows(total)
        sums_ref[16:24, :] += fold_rows(d_h1)
        dh1_ref[...] = d_h1
        low = d_h1.astype(LOW)
        dbr_ref[mine, :] = low
        fetch.wait(tail, tail + 1)
        datt_ref[...] = mm_nt(low, wo_ref[...]).astype(LOW)

    @pl.when(step == steps - 1)
    def _():
        for i in (tail + 2, tail + 3):
            fetch.copies[i].wait()

    wide = ut_ref.shape[2]
    at = steps
    for side in (1, 0):
        for start in range(side * half, (side + 1) * half, wide):

            @pl.when(step == at)
            def _():
                grad = mm_tn(low_ref[...], dpre_ref[:, start : start + wide]).astype(LOW)
                spread(grad, (uo_ref, ut_ref)[side], ALL, table_of(s_ref, 1, side, parts), parts)

            at += 1

    @pl.when(step == at)
    def _():
        grad = mm_tn(dbr_ref[...], att_ref[...]).astype(LOW)
        spread(grad[:, :cols], oo_ref, ALL, table_of(s_ref, 1, 0, parts), parts)
        spread(grad[:, cols:], ot_ref, ALL, table_of(s_ref, 1, 1, parts), parts)


def ffn_bwd(scal, d_mlp, slope, hat, scale, normed_low, att, w_out, w_up, w_down, gain_one, block, chunk, wide, parts):
    rows, width = d_mlp.shape
    steps = rows // block
    half = w_up[0].shape[1]
    pieces = half // wide
    cols = w_out[0].shape[0]
    rows_of = lambda w: pl.BlockSpec((block, w), lambda i, s: (jnp.minimum(i, steps - 1), 0))
    moving = [d_mlp, slope, hat, scale]
    lead = slots_of(width, parts)
    piece_at = lambda k: pl.BlockSpec((*lead, wide), lambda i, s: (0, 0, jnp.clip(i - steps - k * pieces, 0, pieces - 1)))
    return pl.pallas_call(
        functools.partial(ffn_bwd_kernel, block, chunk, parts, steps),
        grid_spec=pltpu.PrefetchScalarGridSpec(
            num_scalar_prefetch=1,
            grid=(steps + 2 * pieces + 1,),
            in_specs=[rows_of(m.shape[1]) for m in moving] + [const_spec(gain_one.shape)] + [ANY] * 8,
            out_specs=[rows_of(width), rows_of(2 * cols), fixed((24, width)), fixed((8, 2 * half))]
            + [piece_at(0), piece_at(1)]
            + [fixed((*lead, cols))] * 2,
            scratch_shapes=[
                pltpu.VMEM((2 * cols, width), LOW),
                pltpu.VMEM((width, 2 * half), LOW),
                pltpu.VMEM((2 * half, width), LOW),
                pltpu.VMEM((rows, width), LOW),
                pltpu.VMEM((rows, 2 * cols), LOW),
                pltpu.SemaphoreType.DMA((4 + 4 * half // chunk,)),
                pltpu.VMEM((rows, 2 * half), LOW),
                pltpu.VMEM((rows, width), LOW),
            ],
        ),
        out_shape=[
            jax.ShapeDtypeStruct((rows, width), F32),
            jax.ShapeDtypeStruct((rows, 2 * cols), LOW),
            jax.ShapeDtypeStruct((24, width), F32),
            jax.ShapeDtypeStruct((8, 2 * half), F32),
        ]
        + [jax.ShapeDtypeStruct((*lead, half), LOW)] * 2
        + [jax.ShapeDtypeStruct((*lead, cols), LOW)] * 2,
        compiler_params=params(48),
        cost_estimate=cost(32),
        name="ffn_bwd",
    )(scal, *moving, gain_one, *w_out, *w_up, *w_down, normed_low, att)


def attn_bwd_kernel(block, side, parts, steps, s_ref, *refs):
    q_ref, k_ref, v_ref, p_ref, da_ref, base_ref, x_hbm, w_hbm = refs[:8]
    if side:
        part_ref, _, sum_ref, grad_ref, tok_ref, whole_ref = refs[8:-5]
    else:
        two_ref, one_ref, bup_ref, other_ref, sum_ref, grad_ref, tok_ref, own_ref, keep_ref, send_ref = refs[8:-5]
    x_ref, w_ref, sems, all_ref, dl_ref = refs[-5:]
    step = pl.program_id(0)
    cols = da_ref.shape[1]
    rows = x_ref.shape[0]
    fetch = Fetch(
        [w_hbm.at[kind] for kind in range(3)] + [x_hbm.at[pl.ds(pl.multiple_of(s_ref[0] * rows, rows), rows)]],
        [w_ref.at[:, kind * cols : (kind + 1) * cols] for kind in range(3)] + [x_ref],
        sems,
    )
    fetch.start()

    @pl.when(step == 0)
    def _():
        sum_ref[...] = jnp.zeros_like(sum_ref)

    @pl.when(step < steps)
    def _():
        if side:
            whole_ref[...] = part_ref[...].astype(whole_ref.dtype)
        masks = head_masks()
        for seg in range(block // SEG):
            at = slice(seg * SEG, (seg + 1) * SEG)
            for pair in range(cols // LANES):
                lanes = slice(pair * LANES, (pair + 1) * LANES)
                k_lanes = slice(cols + pair * LANES, cols + (pair + 1) * LANES)
                v_lanes = slice(2 * cols + pair * LANES, 2 * cols + (pair + 1) * LANES)
                low_probs = p_ref[at, 2 * pair * SEG : 2 * (pair + 1) * SEG]
                probs = low_probs.astype(F32)
                d_att = split_heads(da_ref[at, lanes], masks)
                d_probs = mm_nt(v_ref[at, lanes], d_att)
                d_scores = (probs * (d_probs - jnp.sum(probs * d_probs, 0, keepdims=True))).astype(LOW)
                d_v = mm(low_probs, d_att).astype(LOW)
                d_k = mm(d_scores, split_heads(q_ref[at, lanes], masks)).astype(LOW)
                stacked = jnp.concatenate([d_scores[:, :SEG], d_scores[:, SEG:]], 0)
                d_q = (mm_tn(stacked, split_heads(k_ref[at, lanes], masks)) * (HEAD_DIM**-0.5)).astype(LOW)
                dl_ref[at, lanes] = d_q
                dl_ref[at, k_lanes] = d_k
                dl_ref[at, v_lanes] = d_v
                sum_ref[:, lanes] += fold_rows(d_q.astype(F32))
                sum_ref[:, k_lanes] += fold_rows(d_v.astype(F32))
        all_ref[pl.ds(pl.multiple_of(step * block, block), block), :] = dl_ref[...]
        fetch.wait(0, 1, 2)
        total = base_ref[...] + mm_nt(dl_ref[...], w_ref[...])
        if side:
            tok_ref[...] = total
        else:
            total = total.astype(OWN)
            tok_ref[...] = total.astype(F32)
            own_ref[...] = total

    @pl.when(step == steps)
    def _():
        fetch.copies[3].wait()
        grad = mm_tn(x_ref[...], all_ref[...]).astype(LOW)
        spread(grad, grad_ref, ALL, table_of(s_ref, 0, side, parts), parts)
        if not side:
            half = bup_ref.shape[1] // 2
            width = one_ref.shape[1]
            for to, ref, sum_of in ((0, keep_ref, sum_ref), (1, send_ref, other_ref)):
                ref[...] = jnp.zeros_like(ref)
                at = 0
                pieces = [(norm, 8 * group, 0, width) for norm in (two_ref, one_ref) for group in range(3)]
                pieces += [(bup_ref, 0, to * half, half), (sum_of, 0, 0, 2 * cols)]
                for source, top, start, count in pieces:
                    total = jnp.sum(source[top : top + 8, start : start + count], 0, keepdims=True)
                    for piece in range(count // LANES):
                        ref[at : at + 1, :] = total[:, piece * LANES : (piece + 1) * LANES]
                        at += 1


def attn_bwd(scal, qkv, probs, d_att, base, w, extra, tokens, side, block, parts):
    rows = qkv.shape[0]
    width = tokens.shape[1]
    cols = d_att.shape[1] // 2
    steps = rows // block
    row = lambda i: jnp.minimum(i, steps - 1)
    part_of = lambda w, at: pl.BlockSpec((block, w), lambda i, s: (row(i), at))
    lead = slots_of(width, parts)
    in_specs = [part_of(cols, 2 * kind + side) for kind in range(3)] + [part_of(probs.shape[1] // 2, side), part_of(cols, side)]
    in_specs += [part_of(width, 0), ANY, ANY]
    out_specs = [fixed((8, 2 * cols)), fixed((*lead, 3 * cols))]
    out_shape = [jax.ShapeDtypeStruct((8, 2 * cols), F32), jax.ShapeDtypeStruct((*lead, 3 * cols), LOW)]
    if side:
        in_specs += [part_of(width, 0), ANY]
        out_specs += [part_of(width, 0), pl.BlockSpec((block, width), lambda i, s: ((1 - s[0]) * steps + row(i), 0))]
        out_shape += [jax.ShapeDtypeStruct((rows, width), F32), jax.ShapeDtypeStruct(extra[1].shape, F32)]
    else:
        in_specs += [const_spec(m.shape) for m in extra]
        small = -(-(6 * width + extra[2].shape[1] // 2 + 2 * cols) // (8 * LANES)) * 8
        out_specs += [pl.BlockSpec((block, width), lambda i, s: (s[0] * steps + row(i), 0)), part_of(width, 0)]
        out_specs += [fixed((small, LANES))] * 2
        out_shape += [jax.ShapeDtypeStruct((2 * rows, width), F32), jax.ShapeDtypeStruct((rows, width), OWN)]
        out_shape += [jax.ShapeDtypeStruct((small, LANES), F32)] * 2
    return pl.pallas_call(
        functools.partial(attn_bwd_kernel, block, side, parts, steps),
        grid_spec=pltpu.PrefetchScalarGridSpec(
            num_scalar_prefetch=1,
            grid=(steps + 1,),
            in_specs=in_specs,
            out_specs=out_specs,
            scratch_shapes=[
                pltpu.VMEM((rows, width), LOW),
                pltpu.VMEM((width, 3 * cols), LOW),
                pltpu.SemaphoreType.DMA((4,)),
                pltpu.VMEM((rows, 3 * cols), LOW),
                pltpu.VMEM((block, 3 * cols), LOW),
            ],
        ),
        out_shape=out_shape,
        input_output_aliases={10: 3} if side else {},
        compiler_params=params(30),
        cost_estimate=cost(15),
        name="attn_bwd",
    )(scal, qkv, qkv, qkv, probs, d_att, base, tokens, w, *extra)


def place_kernel(s_ref, whole_ref, part_ref, out_ref):
    out_ref[...] = part_ref[...].astype(out_ref.dtype)


def place_other(scal, whole, piece, block):
    rows, width = piece.shape
    steps = rows // block
    return pl.pallas_call(
        place_kernel,
        grid_spec=pltpu.PrefetchScalarGridSpec(
            num_scalar_prefetch=1,
            grid=(steps,),
            in_specs=[ANY, row_spec(block, width)],
            out_specs=pl.BlockSpec((block, width), lambda i, s: ((1 - s[0]) * steps + i, 0)),
        ),
        out_shape=jax.ShapeDtypeStruct(whole.shape, F32),
        input_output_aliases={1: 0},
        compiler_params=params(16),
        cost_estimate=cost(4),
        name="place_other",
    )(scal, whole, piece)


def shards(
    n_docs, tokens, grad_out, live_tokens, w_qkv, b_qv, w_out, b_out, gain_one, shift_one, w_up, b_up, w_down, b_down,
    gain_two, shift_two,
):
    c = lax.axis_index("heads")
    me = lax.axis_index("docs")
    rows = tokens.shape[0] // 2
    bits = n_docs.bit_length() - 1
    rest = list(range(2, bits))
    orders = [[[0, 1, *rest], [1, 0, *rest]]] * 2

    def step(value, kind, stage):
        pairs = [(d * 2 + h, (d ^ (1 << orders[kind][h][stage])) * 2 + h) for d in range(n_docs) for h in range(2)]
        return lax.ppermute(value, ("docs", "heads"), pairs)

    def swap(value):
        return lax.ppermute(value, "heads", [(0, 1), (1, 0)])

    def after(value, *before):
        return lax.optimization_barrier((value, *before))[0]

    def table_for(kind, core):
        away = jnp.arange(n_docs, dtype=jnp.int32) ^ me
        slots = []
        for order in orders[kind]:
            slot = jnp.zeros((n_docs,), jnp.int32)
            for place, bit in enumerate(order):
                slot = slot | (((away >> bit) & 1) << (bits - 1 - place))
            slots.append(slot)
        return jnp.where(core == 0, slots[0], slots[1])

    tables = [table_for(kind, core) for kind in range(2) for core in (c, 1 - c)]
    scal = jnp.concatenate([c[None].astype(jnp.int32), live_tokens, *tables])

    w_qkv = jnp.transpose(w_qkv, (1, 0, 2))
    w_qkv2 = (w_qkv, swap(w_qkv))
    b_qv2 = (b_qv, swap(b_qv))
    b_up2 = (b_up, swap(b_up))
    w_out, w_up, w_down = after((w_out, w_up, w_down), w_qkv2[1], b_qv2[1], b_up2[1], scal)
    w_out2 = (w_out, swap(w_out))
    w_up2 = (w_up, swap(w_up))
    w_down2 = (w_down, swap(w_down))
    vec = (b_out, gain_one, shift_one, b_down, gain_two, shift_two)

    def add(left, right):
        return (left.astype(F32) + right.astype(F32)).astype(LOW)

    def first_sum(kind, pairs):
        half = n_docs // 2
        parts = [(arrange(own, tables[2 * kind], n_docs), arrange(swap(other), tables[2 * kind], n_docs)) for own, other in pairs]
        cut = lambda at: jnp.concatenate([add(own[at], other[at]) for own, other in parts], 2)
        return cut(slice(half, None)), cut(slice(None, half))

    def next_sum(keep, came):
        half = keep.shape[0] // 2
        if not half:
            return (keep.astype(F32) + came.astype(F32))[0]
        return add(keep[half:], came[half:]), add(keep[:half], came[:half])

    half = w_up.shape[1]
    cols = w_out.shape[0]
    qkv, probs, att = attn_fwd(scal, tokens, w_qkv2, b_qv2, rows, BLOCK)
    def stage_of(kind, pair, stage, *before):
        return next_sum(after(pair[1], *before), step(pair[0], kind, stage))

    layer_out, layer_own, slope, normed_low, hat, scale, d_mlp, sums_two, down_other, down_own = ffn_fwd(
        scal, tokens, grad_out, att, w_out2, w_up2, b_up2, w_down2, vec, rows, BLOCK, FF_CHUNK, 768, n_docs
    )
    down = first_sum(0, [(down_own, down_other)])
    d_mlp = after(d_mlp, down[0])
    d_h1, d_att, sums_one, sums_up, up_other, up_own, out_other, out_own = ffn_bwd(
        scal, d_mlp, slope, hat, scale, normed_low, att, w_out2, w_up2, w_down2, gain_one, BLOCK, FF_CHUNK, 768, n_docs
    )
    down = stage_of(0, down, 0, up_own)
    up_own, out_own, out_other, layer_own = after((up_own, out_own, out_other, layer_own), down[0])
    up = first_sum(1, [(up_own, up_other), (out_own, out_other)])
    sums_other, qkv_other, d_tokens, layer_out = attn_bwd(
        scal, qkv, probs, after(d_att, *up), d_h1, w_qkv2[1], (swap(layer_own), layer_out), tokens, 1, BLOCK, n_docs
    )
    down = stage_of(0, down, 1, qkv_other)
    qkv_other, keep_up = after((qkv_other, up[1]), down[0])
    up = stage_of(1, (up[0], keep_up), 0)
    sums = (sums_two, sums_one, sums_up, sums_other)
    _, qkv_own, d_tokens, tokens_own, small_keep, small_send = attn_bwd(
        scal, qkv, probs, after(d_att, up[0]), d_tokens, w_qkv2[0], sums, tokens, 0, BLOCK, n_docs
    )

    def spread_small(small, stage, *before):
        pairs = [(d, d ^ (1 << stage)) for d in range(n_docs)]
        return after(small, *before) + lax.ppermute(small, "docs", pairs)

    down = stage_of(0, down, 2, qkv_own)
    lin = first_sum(0, [(after(qkv_own, down[0]), qkv_other)])
    up = stage_of(1, up, 1, lin[0])
    small = after(small_keep, up[0]) + swap(after(small_send, down[0]))
    lin = stage_of(0, lin, 0, small)
    d_tokens = place_other(scal, after(d_tokens, lin[0]), swap(after(tokens_own, down[0])), 2 * BLOCK)
    small = spread_small(small, 0, d_tokens)
    up = stage_of(1, up, 2, small)
    last = up[0]
    for stage in range(1, bits - 1):
        lin = stage_of(0, lin, stage, last)
        if stage + 2 < bits:
            down = stage_of(0, down, stage + 2, lin[0])
        if stage + 3 < bits:
            up = stage_of(1, up, stage + 2, down[0])
        if stage == bits - 2:
            up = stage_of(1, up, bits - 1, lin[0])
        small = spread_small(small, stage, up[0], down[0])
        last = small
    small = spread_small(small, bits - 1, up)
    lin = stage_of(0, lin, bits - 1, small)
    d_w_down = down.T
    d_w_up, d_w_out = up[:, :half], up[:, half:].T
    d_w_qkv = lin.reshape(-1, 3, cols)
    small = small.reshape(-1)
    width = tokens.shape[1]
    d_gain_two, d_shift_two, d_b_down, d_gain_one, d_shift_one, d_b_out = (
        small[i * width : (i + 1) * width] for i in range(6)
    )
    d_b_up = small[6 * width : 6 * width + half]
    d_b_qv = small[6 * width + half : 7 * width + half].reshape(2, cols)
    return (
        layer_out,
        d_tokens,
        d_w_qkv,
        d_b_qv,
        d_w_out,
        d_b_out,
        d_gain_one,
        d_shift_one,
        d_w_up,
        d_b_up,
        d_w_down,
        d_b_down,
        d_gain_two,
        d_shift_two,
    )


def solution(mesh):
    placed = (
        P("docs", None),
        P("docs", None),
        P("docs"),
        P(None, None, "heads"),
        P(None, "heads"),
        P("heads", None),
        P(),
        P(),
        P(),
        P(None, "heads"),
        P("heads"),
        P("heads", None),
        P(),
        P(),
        P(),
    )
    return jax.shard_map(
        functools.partial(shards, mesh.shape["docs"]),
        mesh=mesh,
        in_specs=placed,
        out_specs=(
            P("docs", None),
            P("docs", None),
            P("docs", None, "heads"),
            P(None, "heads"),
            P("heads", "docs"),
            P(),
            P(),
            P(),
            P("docs", "heads"),
            P("heads"),
            P("heads", "docs"),
            P(),
            P(),
            P(),
        ),
        check_vma=False,
    )
```
